256 devices in a mesh: gx: 16 (over z, core), gy: 4 (over x), gz: 4 (over y).
Axes of the slice: x: 4, y: 4, z: 8, core: 2. Of those that a mesh axis runs over, the one named last changes fastest.
Arguments:
- heights: float32 [8192, 8192], P(('gy', 'gz'), 'gx'), may hold values from -6 to 6
- scene_ids: int32 [8192, 8192], P(('gy', 'gz'), 'gx'), may hold values from 0 to 15, as said below
- scene_offset: float32 [16], replicated, may hold values from -4 to 4
- scene_weight: float32 [16], replicated, may hold values from 0.2 to 5
- band_gain: float32 [6], replicated, may hold values from 0.3 to 1.5
Outputs:
- blended: float32 [8192, 8192], P(('gy', 'gz'), 'gx')
The draws below stay inside these ranges and needn't reach their ends.
Inputs may be any that keep to these rules, and one draw needn't show every extreme that they name: `scene_ids`: scene index of each cell.
All inputs are finite; a program needn't handle non-finite values.
Results may differ from the reference program's by a relative error of at most 0.00002.
Values sent between devices are 32-bit elements; how exact they have to be, the bound alone decides.
No kernel may reach another device: no remote copies, remote signals or barrier semaphores. Data moves between devices by JAX's collectives and lax.ppermute only.
A program may use at most 128 MiB of HBM per device.

```python
import math
import jax
import jax.numpy as jnp

SCENES = 16
LEVELS = 6
NR = 8192
NC = 8192


def draw_scene_ids(key, part):
    key_grid = jax.random.fold_in(key, 11)
    key_jitter = jax.random.fold_in(key, 23)
    grid = jax.random.randint(key_grid, (NR // 48 + 2, NC // 48 + 2), 0, SCENES).astype(jnp.int32)
    grid = grid.at[0, 0].set(SCENES - 1).at[0, 1].set(0)
    jitter = jax.random.randint(key_jitter, (NR,), 0, 16).astype(jnp.int32)
    row_cell = (jnp.arange(NR, dtype=jnp.int32) // 48)[:, None]
    col_cell = (jnp.arange(NC, dtype=jnp.int32)[None, :] + jitter[:, None]) // 48
    return grid[row_cell, col_cell].astype(jnp.int32)


def shard_levels(stream_key, extent, split, least, top_value):
    def one(dim, shards_of):
        steps = jax.random.uniform(jax.random.fold_in(jax.random.fold_in(stream_key, 6), dim), (shards_of,), jnp.float32, least / len(split), top_value / len(split))
        return jnp.repeat(jnp.exp(steps), extent[dim] // shards_of).reshape((-1,) + (1,) * (len(extent) - dim - 1))

    factor_of = one(*split[0])
    for cut in split[1:]:
        factor_of = factor_of * one(*cut)
    return factor_of


def gaussian(stream_key, dims, scale, bound, cuts=(), kind=jnp.bfloat16):
    values = scale * jax.random.normal(stream_key, dims, jnp.float32)
    if cuts:
        values = values * shard_levels(stream_key, dims, cuts, -0.22, 0.18)
    return jnp.clip(values, -bound, bound).astype(kind)


def setup_inputs(seed: int = 0) -> dict:
    key_of = jax.random.split(jax.random.key(seed), 6)
    return {
        "heights": gaussian(key_of[0], (NR, NC), 1.0, 6.0, ((0, 16), (1, 16)), jnp.float32),
        "scene_ids": draw_scene_ids(jax.random.fold_in(key_of[5], 71), 0),
        "scene_offset": jnp.clip(jax.random.uniform(key_of[2], (SCENES,), jnp.float32, -4.0, 4.0), -4.0, 4.0),
        "scene_weight": jnp.clip(jnp.exp(jax.random.uniform(key_of[3], (SCENES,), jnp.float32, math.log(0.2), math.log(5.0))), 0.2, 5.0),
        "band_gain": jnp.clip(jnp.exp(jax.random.uniform(key_of[4], (LEVELS,), jnp.float32, math.log(0.3), math.log(1.5))), 0.3, 1.5),
    }


KERN = (0.0625, 0.25, 0.375, 0.25, 0.0625)


def lookup(scene_ids, table):
    acc = jnp.zeros(scene_ids.shape, jnp.float32)
    for scene in range(SCENES):
        acc = acc + jnp.where(scene_ids == scene, table[scene], jnp.float32(0.0))
    return acc


def reduce_padded(padded):
    rows_out = padded.shape[-2] - 4
    cols_out = padded.shape[-1] - 4
    rows = KERN[0] * padded[..., 0:rows_out:2, :]
    for tap in range(1, 5):
        rows = rows + KERN[tap] * padded[..., tap:tap + rows_out:2, :]
    result = KERN[0] * rows[..., 0:cols_out:2]
    for tap in range(1, 5):
        result = result + KERN[tap] * rows[..., tap:tap + cols_out:2]
    return result


def expand_padded(padded):
    count = padded.shape[-2] - 2
    even = (padded[..., 0:count, :] + 6.0 * padded[..., 1:count + 1, :] + padded[..., 2:count + 2, :]) * 0.125
    odd = (padded[..., 1:count + 1, :] + padded[..., 2:count + 2, :]) * 0.5
    rows = jnp.stack([even, odd], axis=-2)
    rows = rows.reshape(rows.shape[:-3] + (2 * count, rows.shape[-1]))
    width = rows.shape[-1] - 2
    even = (rows[..., 0:width] + 6.0 * rows[..., 1:width + 1] + rows[..., 2:width + 2]) * 0.125
    odd = (rows[..., 1:width + 1] + rows[..., 2:width + 2]) * 0.5
    result = jnp.stack([even, odd], axis=-1)
    return result.reshape(result.shape[:-2] + (2 * width,))


def reference(heights, scene_ids, scene_offset, scene_weight, band_gain):
    weight = lookup(scene_ids, scene_weight)
    offset = lookup(scene_ids, scene_offset)
    numer = weight * (heights + offset)
    denom = weight
    ratios = [numer / denom]
    for level in range(LEVELS):
        numer = reduce_padded(jnp.pad(numer, 2))
        denom = reduce_padded(jnp.pad(denom, 2))
        ratios.append(numer / denom)
    top_mean = jnp.sum(numer) / jnp.sum(denom)
    collapsed = jnp.zeros_like(ratios[LEVELS]) + top_mean
    for level in range(LEVELS - 1, -1, -1):
        band = ratios[level] - expand_padded(jnp.pad(ratios[level + 1], 1))
        collapsed = band_gain[level] * band + expand_padded(jnp.pad(collapsed, 1))
    return collapsed
```

```python
import jax
import jax.numpy as jnp
import numpy as np
from jax import lax
from jax.experimental import pallas as pl
from jax.experimental.pallas import tpu as pltpu
from jax.sharding import PartitionSpec as P

SCENES = 16
LEVELS = 6
TILE = 512
KERN = (0.0625, 0.25, 0.375, 0.25, 0.0625)
ROWS = ("gy", "gz")
COLS = "gx"

N = [TILE >> level for level in range(LEVELS + 1)]
R = [0, 272, 144, 80, 48, 32, 32]
A = [560, 304, 176, 112, 80, 80, 40]
W = [512, 384, 256, 128, 128, 128, 128]
STRIP = [0, 0, 384, 640, 768, 896, 1024]
STRIPS = 1152
BLOCK = [0, 0, 272, 416, 496, 544, 576]
BLOCKS = 608
HIGH = [0, 256, 128, 0, 0, 0, 0]
TURN = [0, 0, 0, 64, 96, 112, 120]
VMEM = 40 * 1024 * 1024


def reduce_matrix(rows, cols, shift):
    out = np.zeros((rows, cols), np.float32)
    for s in range(cols):
        for tap in range(5):
            t = 2 * s - 2 - shift + tap
            if 0 <= t < rows:
                out[t, s] = KERN[tap]
    return out.astype(jnp.bfloat16)


def expand_matrix(rows, cols, shift):
    out = np.zeros((rows, cols), np.float32)
    for c in range(cols):
        s = c + shift
        j = s // 2
        taps = ((j, 0.5), (j + 1, 0.5)) if s % 2 == 0 else ((j, 0.125), (j + 1, 0.75), (j + 2, 0.125))
        for t, value in taps:
            if 0 <= t < rows:
                out[t, c] = value
    return out.astype(jnp.bfloat16)


def times(x, matrix):
    hi = x.astype(jnp.bfloat16)
    rest = x - hi.astype(jnp.float32)
    mid = rest.astype(jnp.bfloat16)
    lo = (rest - mid.astype(jnp.float32)).astype(jnp.bfloat16)
    out = jnp.dot(hi, matrix, preferred_element_type=jnp.float32)
    out = out + jnp.dot(mid, matrix, preferred_element_type=jnp.float32)
    return out + jnp.dot(lo, matrix, preferred_element_type=jnp.float32)


def load(ref, arr, at):
    return jnp.concatenate([ref[arr, tile, at, :] for tile in range(ref.shape[1])], axis=1)


def store(ref, arr, at, value):
    for tile in range(value.shape[1] // 128):
        ref[arr, tile, at, :] = value[:, 128 * tile : 128 * tile + 128]


def row_place():
    return lax.axis_index("gy") * lax.axis_size("gz") + lax.axis_index("gz")


def in_grid(shape, n, rows, cols):
    def side(dim, place, count):
        s = lax.broadcasted_iota(jnp.int32, shape, dim)
        low = jnp.where(place == 0, 1, 0)
        high = jnp.where(place == count - 1, n, n + 2)
        return (s >= low) & (s <= high)

    return side(0, row_place(), rows) & side(1, lax.axis_index(COLS), cols)


def halves(num, den):
    lane = lax.broadcasted_iota(jnp.int32, num.shape, 1)
    return jnp.where(lane < 64, num, den)


def roll(x, shift, axis):
    return pltpu.roll(x, shift % x.shape[axis], axis) if shift % x.shape[axis] else x


def pyramid(rows, cols, offset, weight, heights, ids, first, later, shifted, *refs):
    levels, (low_cols, high_cols, message, base) = refs[:LEVELS], refs[LEVELS:]
    step = 32
    for arr in range(2):
        store(base, arr, slice(0, 8), jnp.zeros((8, TILE), jnp.float32))
        store(base, arr, slice(8 + TILE, A[0]), jnp.zeros((A[0] - 8 - TILE, TILE), jnp.float32))

    def cells(i, _):
        at = pl.ds(pl.multiple_of(i * step, step), step)
        to = pl.ds(pl.multiple_of(i * step + 8, 8), step)
        which = ids[at, :]
        bits = [(which & (1 << b)) != 0 for b in range(4)]

        def lookup(table):
            values = [table[s] for s in range(SCENES)]
            for b in range(4):
                values = [
                    jnp.where(bits[b], values[2 * k + 1], values[2 * k]) for k in range(len(values) // 2)
                ]
            return values[0]

        w = lookup(weight)
        h = heights[at, :] + lookup(offset)
        shifted[at, :] = h
        store(base, 0, to, w * h)
        store(base, 1, to, w)
        return 0

    lax.fori_loop(0, TILE // step, cells, 0)

    for level in range(1, LEVELS + 1):
        source = base if level == 1 else levels[level - 2]
        target = levels[level - 1]
        start = 4 if level == 1 else 5
        size = R[level]
        matrix = first[...] if level == 1 else later[: W[level - 1], : W[level]]
        mask = in_grid((size, W[level]), N[level], rows, cols)
        for arr in range(2):
            taps = [load(source, arr, pl.ds(start + k, size, stride=2)) for k in range(5)]
            tall = KERN[0] * (taps[0] + taps[4]) + KERN[1] * (taps[1] + taps[3]) + KERN[2] * taps[2]
            part = jnp.where(mask, times(tall, matrix), 0.0)
            store(target, arr, slice(0, 8), jnp.zeros((8, W[level]), jnp.float32))
            store(target, arr, slice(8, 8 + size), part)
            if A[level] > 8 + size:
                rest = A[level] - 8 - size
                store(target, arr, slice(8 + size, A[level]), jnp.zeros((rest, W[level]), jnp.float32))

    row = row_place()
    sub = lax.broadcasted_iota(jnp.int32, (8, 128), 0)
    message[...] = jnp.zeros(message.shape, jnp.float32)
    totals = [jnp.sum(levels[LEVELS - 1][arr, 0, 8 : 8 + R[LEVELS], :]) for arr in range(2)]
    plain = jnp.where(sub == 3, totals[0], jnp.where(sub == 7, totals[1], 0.0))

    def strips(level, at):
        ref = levels[level - 1]
        num = load(ref, 0, slice(at, at + 8))
        den = pltpu.roll(load(ref, 1, slice(at, at + 8)), 4, 0)
        sub = lax.broadcasted_iota(jnp.int32, num.shape, 0)
        return jnp.where(sub < 3, num, jnp.where((sub > 3) & (sub < 7), den, 0.0))

    top = STRIP[LEVELS]
    for slot in range(rows):
        message[slot, :, top : top + 128] = plain

    @pl.when(row > 0)
    def _():
        for level in range(1, LEVELS + 1):
            packed = strips(level, 8)
            if level == LEVELS:
                packed = packed + plain
            message[row - 1, :, STRIP[level] : STRIP[level] + W[level]] = packed

    @pl.when(row < rows - 1)
    def _():
        for level in range(1, LEVELS + 1):
            packed = strips(level, 8 + N[level])
            if level == LEVELS:
                packed = packed + plain
            message[row + 1, :, STRIP[level] : STRIP[level] + W[level]] = packed

    for level in range(1, LEVELS + 1):
        size, high, turn = R[level], HIGH[level] // 128, TURN[level]
        ref = levels[level - 1]
        to = slice(BLOCK[level], BLOCK[level] + size)
        low_cols[to, :] = halves(ref[0, 0, 8 : 8 + size, :], roll(ref[1, 0, 8 : 8 + size, :], 64, 1))
        high_cols[to, :] = halves(
            roll(ref[0, high, 8 : 8 + size, :], turn, 1),
            roll(ref[1, high, 8 : 8 + size, :], turn + 64, 1),
        )


def from_rows(rows, message, level):
    row = row_place()
    out = []
    for place in (row - 1, row + 1):
        there = (place >= 0) & (place < rows)
        got = message[jnp.clip(place, 0, rows - 1), :, STRIP[level] : STRIP[level] + W[level]]
        sub = lax.broadcasted_iota(jnp.int32, got.shape, 0)
        keep = (sub < 3) & there
        out.append((jnp.where(keep, got, 0.0), jnp.where(keep, pltpu.roll(got, 4, 0), 0.0)))
    return out


def edges(rows, cols, low_in, high_in, message, low_out, high_out, totals):
    low_out[...] = low_in[...]
    high_out[...] = high_in[...]
    for level in range(1, LEVELS + 1):
        high, turn = HIGH[level], TURN[level]
        for at, (num, den) in zip((0, N[level]), from_rows(rows, message, level)):
            to = slice(BLOCK[level] + at, BLOCK[level] + at + 8)
            low_out[to, :] += halves(num[:, 0:128], roll(den[:, 0:128], 64, 1))
            high_out[to, :] += halves(
                roll(num[:, high : high + 128], turn, 1), roll(den[:, high : high + 128], turn + 64, 1)
            )
    top = STRIP[LEVELS]
    total = message[0, :, top : top + 128]
    for slot in range(1, rows):
        total = total + message[slot, :, top : top + 128]
    both = halves(total[3:4, :], total[7:8, :])
    for slot in range(cols):
        totals[slot, :, :] = both


def collapse(rows, cols, gain, l1, l2, l3, l4, l5, l6, message, below, above, totals, wider, last, shifted, out, tall, wide, full):
    levels = (l1, l2, l3, l4, l5, l6)
    total = totals[0, :, :]
    for slot in range(1, cols):
        total = total + totals[slot, :, :]
    mean = total[0:1, 0:1] / total[0:1, 64:65]

    def ratio(level):
        size, n, high = R[level], N[level], HIGH[level] // 128
        ref = levels[level - 1]
        strips = from_rows(rows, message, level)
        lane = lax.broadcasted_iota(jnp.int32, (size, 128), 1)
        at = slice(BLOCK[level], BLOCK[level] + size)
        for arr in range(2):
            store(full, arr, slice(0, size), load(ref, arr, slice(8, 8 + size)))
            for first, pair in zip((0, n), strips):
                for tile in range(W[level] // 128):
                    full[arr, tile, first : first + 8, :] += pair[arr][:, 128 * tile : 128 * tile + 128]
            low = jnp.where(lane < 3, roll(below[at, :], 64 * arr, 1), 0.0)
            up = jnp.where(lane < 3, roll(above[at, :], 64 * arr, 1), 0.0)
            full[arr, 0, 0:size, :] += low
            full[arr, high, 0:size, :] += roll(up, n, 1)
        mask = in_grid((size, W[level]), n, rows, cols)
        num, den = (load(full, arr, slice(0, size))[:, : W[level]] for arr in range(2))
        return mask, jnp.where(mask, num / jnp.where(mask, den, 1.0), 0.0)

    mask, value = ratio(LEVELS)
    piece = jnp.where(mask, mean - gain[LEVELS - 1] * value, 0.0)
    for level in range(LEVELS - 1, 0, -1):
        size, half = R[level], R[level] // 2
        tall[0 : R[level + 1], 0 : W[level]] = times(piece, wider[: W[level + 1], : W[level]])
        a, b, c = (tall[k : k + half, 0 : W[level]] for k in range(3))
        mask, value = ratio(level)
        even, odd = 0.5 * (a + b), 0.125 * (a + c) + 0.75 * b
        for tile in range(W[level] // 128):
            lanes = slice(128 * tile, 128 * tile + 128)
            wide[tile, pl.ds(0, half, stride=2), :] = even[:, lanes]
            wide[tile, pl.ds(1, half, stride=2), :] = odd[:, lanes]
        grown = jnp.concatenate([wide[tile, 0:size, :] for tile in range(W[level] // 128)], axis=1)
        change = gain[level] - gain[level - 1]
        piece = jnp.where(mask, change * value + grown, 0.0)
    tall[...] = times(piece, last[...])
    half = TILE // 2
    for tile in range(W[0] // 128):
        lanes = slice(128 * tile, 128 * tile + 128)
        a, b, c = (tall[k : k + half, lanes] for k in range(3))
        wide[tile, pl.ds(0, half, stride=2), :] = 0.125 * (a + c) + 0.75 * b
        wide[tile, pl.ds(1, half, stride=2), :] = 0.5 * (b + c)
        out[:, lanes] = gain[0] * shifted[:, lanes] + wide[tile, :, :]


def solution(mesh):
    rows, cols = mesh.shape["gy"] * mesh.shape["gz"], mesh.shape["gx"]
    first = reduce_matrix(W[0], W[1], 2)
    later = reduce_matrix(W[1], W[2], 1)
    wider = expand_matrix(W[2], W[1], 0)
    last = expand_matrix(W[1], W[0], 1)
    f32 = jnp.float32
    smem, vmem = pl.BlockSpec(memory_space=pltpu.SMEM), pl.BlockSpec(memory_space=pltpu.VMEM)
    params = pltpu.CompilerParams(vmem_limit_bytes=VMEM)
    stored = [jax.ShapeDtypeStruct((2, W[level] // 128, A[level], 128), f32) for level in range(1, LEVELS + 1)]
    block = jax.ShapeDtypeStruct((BLOCKS, 128), f32)

    def local(heights, ids, offset, weight, gain):
        shifted, *rest = pl.pallas_call(
            lambda *refs: pyramid(rows, cols, *refs),
            out_shape=[jax.ShapeDtypeStruct((TILE, TILE), f32), *stored, block, block]
            + [jax.ShapeDtypeStruct((rows, 8, STRIPS), f32)],
            in_specs=[smem, smem] + [vmem] * 4,
            out_specs=[vmem] * 10,
            scratch_shapes=[pltpu.VMEM((2, W[0] // 128, A[0], 128), f32)],
            compiler_params=params,
            name="pyramid",
        )(offset, weight, heights, ids, first, later)
        levels, (low, high, message) = rest[:LEVELS], rest[LEVELS:]
        message = lax.all_to_all(message, ROWS, 0, 0)
        low, high, totals = pl.pallas_call(
            lambda *refs: edges(rows, cols, *refs),
            out_shape=[block, block, jax.ShapeDtypeStruct((cols, 1, 128), f32)],
            in_specs=[vmem] * 3,
            out_specs=[vmem] * 3,
            compiler_params=params,
            name="edges",
        )(low, high, message)
        above = lax.ppermute(low, COLS, [(i + 1, i) for i in range(cols - 1)])
        below = lax.ppermute(high, COLS, [(i, i + 1) for i in range(cols - 1)])
        totals = lax.all_to_all(totals, COLS, 0, 0)
        return pl.pallas_call(
            lambda *refs: collapse(rows, cols, *refs),
            out_shape=jax.ShapeDtypeStruct((TILE, TILE), f32),
            in_specs=[smem] + [vmem] * 13,
            out_specs=vmem,
            scratch_shapes=[pltpu.VMEM((R[1], TILE), f32), pltpu.VMEM((W[0] // 128, TILE, 128), f32)]
            + [pltpu.VMEM((2, W[1] // 128, R[1], 128), f32)],
            compiler_params=params,
            name="collapse",
        )(gain, *levels, message, below, above, totals, wider, last, shifted)

    spec = P(ROWS, COLS)
    return jax.shard_map(
        local, mesh=mesh, in_specs=(spec, spec, P(), P(), P()), out_specs=spec, check_vma=False
    )
```

```python
import jax
import jax.numpy as jnp
import numpy as np
from jax import lax
from jax.experimental import pallas as pl
from jax.experimental.pallas import tpu as pltpu
from jax.sharding import PartitionSpec as P

SCENES = 16
LEVELS = 6
TILE = 512
KERN = (0.0625, 0.25, 0.375, 0.25, 0.0625)
ROWS = ("gy", "gz")
COLS = "gx"

N = [TILE >> level for level in range(LEVELS + 1)]
R = [0, 272, 144, 80, 48, 32, 32]
A = [560, 304, 176, 112, 80, 80, 40]
W = [512, 384, 256, 128, 128, 128, 128]
STRIP = [0, 0, 384, 640, 768, 896, 1024]
STRIPS = 1280
SLOT = 80
PIECES = [
    (1, 0, 80, 0, 0),
    (1, 80, 80, 1, 0),
    (1, 160, 80, 2, 0),
    (1, 240, 32, 3, 0),
    (6, 0, 32, 3, 32),
    (2, 0, 80, 4, 0),
    (2, 80, 64, 5, 0),
    (3, 0, 80, 6, 0),
    (4, 0, 48, 7, 0),
    (5, 0, 32, 7, 48),
]
ENDS = 336
HIGH = [0, 256, 128, 0, 0, 0, 0]
TURN = [0, 0, 0, 64, 96, 112, 120]
PARTS = 4
VMEM = 40 * 1024 * 1024
FIRST_VMEM = 203 * 256 * 1024


def reduce_matrix(rows, cols, shift):
    t = lax.broadcasted_iota(jnp.int32, (rows, cols), 0)
    s = lax.broadcasted_iota(jnp.int32, (rows, cols), 1)
    d = jnp.abs(t - 2 * s + shift)
    out = jnp.where(d == 2, KERN[0], 0.0)
    return jnp.where(d == 1, KERN[1], jnp.where(d == 0, KERN[2], out)).astype(jnp.bfloat16)


def expand_matrix(rows, cols, shift):
    out = np.zeros((rows, cols), np.float32)
    for c in range(cols):
        s = c + shift
        j = s // 2
        taps = ((j, 0.5), (j + 1, 0.5)) if s % 2 == 0 else ((j, 0.125), (j + 1, 0.75), (j + 2, 0.125))
        for t, value in taps:
            if 0 <= t < rows:
                out[t, c] = value
    return out.astype(jnp.bfloat16)


def with_ends(matrix):
    for k, x in enumerate((*end_vectors(), np.ones(TILE, np.float32))):
        for part in range(3):
            matrix[ENDS + 3 * k + part] = x.astype(jnp.bfloat16)
            x = x - x.astype(jnp.bfloat16).astype(np.float32)
    return matrix


def times(x, matrix):
    hi = x.astype(jnp.bfloat16)
    rest = x - hi.astype(jnp.float32)
    mid = rest.astype(jnp.bfloat16)
    lo = (rest - mid.astype(jnp.float32)).astype(jnp.bfloat16)
    out = jnp.dot(hi, matrix, preferred_element_type=jnp.float32)
    out = out + jnp.dot(mid, matrix, preferred_element_type=jnp.float32)
    return out + jnp.dot(lo, matrix, preferred_element_type=jnp.float32)


def load(ref, arr, at):
    return jnp.concatenate([ref[arr, tile, at, :] for tile in range(ref.shape[1])], axis=1)


def store(ref, arr, at, value):
    for tile in range(value.shape[1] // 128):
        ref[arr, tile, at, :] = value[:, 128 * tile : 128 * tile + 128]


def row_place():
    return lax.axis_index("gy") * lax.axis_size("gz") + lax.axis_index("gz")


def in_grid(shape, n, rows, cols):
    def side(dim, place, count):
        s = lax.broadcasted_iota(jnp.int32, shape, dim)
        low = jnp.where(place == 0, 1, 0)
        high = jnp.where(place == count - 1, n, n + 2)
        return (s >= low) & (s <= high)

    return side(0, row_place(), rows) & side(1, lax.axis_index(COLS), cols)


def roll(x, shift, axis):
    return pltpu.roll(x, shift % x.shape[axis], axis) if shift % x.shape[axis] else x


def three(num, den, low_slot):
    lane = lax.broadcasted_iota(jnp.int32, num.shape, 1)
    at = 8 * low_slot
    num = jnp.where((lane >= at) & (lane < at + 3), roll(num, at, 1), 0.0)
    return jnp.where((lane >= at + 64) & (lane < at + 67), roll(den, at + 64, 1), num)


def pyramid(rows, cols, heights_in, ids_in, tables, shifted, *refs):
    levels, refs = refs[:LEVELS], refs[LEVELS:]
    low_cols, high_cols, even_rows, odd_rows, totals, gains, base = refs[:7]
    heights, ids, first, later, table, sems = refs[7:]
    step, part = 32, TILE // PARTS
    pairs = [(tables, table)]
    for k in range(PARTS):
        at = slice(k * part, k * part + part)
        pairs.append((heights_in.at[at], heights.at[at]))
        pairs.append((ids_in.at[at], ids.at[at]))
    copies = [pltpu.make_async_copy(a, b, sems.at[k]) for k, (a, b) in enumerate(pairs)]
    for copy in copies:
        copy.start()
    first[...] = reduce_matrix(W[0], W[1], 2)
    later[...] = reduce_matrix(W[1], W[2], 1)
    for arr in range(2):
        store(base, arr, slice(0, 8), jnp.zeros((8, TILE), jnp.float32))
        store(base, arr, slice(8 + TILE, A[0]), jnp.zeros((A[0] - 8 - TILE, TILE), jnp.float32))

    def cells(i, _):
        at = pl.ds(pl.multiple_of(i * step, step), step)
        to = pl.ds(pl.multiple_of(i * step + 8, 8), step)
        which = ids[at, :]
        bits = [(which & (1 << b)) != 0 for b in range(4)]

        def lookup(which_table):
            values = [table[which_table, s] for s in range(SCENES)]
            for b in range(4):
                values = [
                    jnp.where(bits[b], values[2 * k + 1], values[2 * k]) for k in range(len(values) // 2)
                ]
            return values[0]

        w = lookup(1)
        h = heights[at, :] + lookup(0)
        shifted[at, :] = h
        store(base, 0, to, w * h)
        store(base, 1, to, w)
        return 0

    copies[0].wait()
    for k in range(PARTS):
        copies[1 + 2 * k].wait()
        copies[2 + 2 * k].wait()
        lax.fori_loop(k * part // step, (k + 1) * part // step, cells, 0)

    for level in range(1, LEVELS + 1):
        source = base if level == 1 else levels[level - 2]
        target = levels[level - 1]
        start = 4 if level == 1 else 5
        size = R[level]
        matrix = first[...] if level == 1 else later[: W[level - 1], : W[level]]
        mask = in_grid((size, W[level]), N[level], rows, cols)
        for arr in range(2):
            taps = [load(source, arr, pl.ds(start + k, size, stride=2)) for k in range(5)]
            tall = KERN[0] * (taps[0] + taps[4]) + KERN[1] * (taps[1] + taps[3]) + KERN[2] * taps[2]
            part = jnp.where(mask, times(tall, matrix), 0.0)
            store(target, arr, slice(0, 8), jnp.zeros((8, W[level]), jnp.float32))
            store(target, arr, slice(8, 8 + size), part)
            if A[level] > 8 + size:
                rest = A[level] - 8 - size
                store(target, arr, slice(8 + size, A[level]), jnp.zeros((rest, W[level]), jnp.float32))

    even = row_place() % 2 == 0
    lane = lax.broadcasted_iota(jnp.int32, (8, 128), 1)
    sub = lax.broadcasted_iota(jnp.int32, (8, 128), 0)
    sums = [jnp.sum(levels[LEVELS - 1][arr, 0, 8 : 8 + R[LEVELS], :]) for arr in range(2)]
    both = jnp.where(lane < 64, sums[0], sums[1])
    totals[...] = both
    even_rows[:, STRIPS - 128 :] = both
    odd_rows[:, STRIPS - 128 :] = both
    gains[...] = sum(jnp.where(sub == k, table[2, k], 0.0) for k in range(LEVELS))

    def strips(level, at):
        ref = levels[level - 1]
        num = load(ref, 0, slice(at, at + 8))
        den = pltpu.roll(load(ref, 1, slice(at, at + 8)), 4, 0)
        sub = lax.broadcasted_iota(jnp.int32, num.shape, 0)
        return jnp.where(sub < 3, num, jnp.where((sub > 3) & (sub < 7), den, 0.0))

    for level in range(1, LEVELS + 1):
        low, high = strips(level, 8), strips(level, 8 + N[level])
        to = slice(STRIP[level], STRIP[level] + W[level])
        even_rows[:, to] = jnp.where(even, high, low)
        odd_rows[:, to] = jnp.where(even, low, high)

    low_cols[...] = jnp.zeros(low_cols.shape, jnp.float32)
    high_cols[...] = jnp.zeros(high_cols.shape, jnp.float32)
    for level, row, size, slot, place in PIECES:
        tile, turn = HIGH[level] // 128, TURN[level]
        num, den = levels[level - 1].at[0], levels[level - 1].at[1]
        at, to = slice(8 + row, 8 + row + size), slice(place, place + size)
        low_cols[to, :] += three(num[0, at, :], den[0, at, :], slot)
        high_cols[to, :] += three(roll(num[tile, at, :], turn, 1), roll(den[tile, at, :], turn, 1), slot)


def from_rows(rows, even_rows, odd_rows, level):
    even = row_place() % 2 == 0
    to = slice(STRIP[level], STRIP[level] + W[level])
    one, two = even_rows[:, to], odd_rows[:, to]
    near = lax.broadcasted_iota(jnp.int32, one.shape, 0) < 3
    out = []
    row = row_place()
    above = (jnp.where(even, two, one), row > 0)
    below = (jnp.where(even, one, two), row < rows - 1)
    for got, there in (above, below):
        keep = near & there
        out.append((jnp.where(keep, got, 0.0), jnp.where(keep, pltpu.roll(got, 4, 0), 0.0)))
    return out


def edges(rows, low_in, high_in, even_rows, odd_rows, totals, even_cols, odd_cols, low, high):
    low[...] = low_in[...]
    high[...] = high_in[...]
    for level in range(1, LEVELS + 1):
        tile, turn = HIGH[level], TURN[level]
        for at, (num, den) in zip((0, N[level]), from_rows(rows, even_rows, odd_rows, level)):
            for which, row, size, slot, place in PIECES:
                if which == level and row <= at < row + size:
                    to = slice(place + at - row, place + at - row + 8)
                    low[to, :] += three(num[:, 0:128], den[:, 0:128], slot)
                    num, den = (roll(x[:, tile : tile + 128], turn, 1) for x in (num, den))
                    high[to, :] += three(num, den, slot)
    even = lax.axis_index(COLS) % 2 == 0
    one, two = low[...], high[...]
    even_cols[0:SLOT, :] = jnp.where(even, two, one)
    odd_cols[0:SLOT, :] = jnp.where(even, one, two)
    even_cols[SLOT:, :] = totals[...]
    odd_cols[SLOT:, :] = totals[...]


def collapse(rows, cols, gains, l1, l2, l3, l4, l5, l6, even_rows, odd_rows, even_cols, odd_cols, wider, last, shifted, out, field, tall, wide, full):
    levels = (l1, l2, l3, l4, l5, l6)
    first_of_pair = lax.axis_index(COLS) % 2 == 0
    gain = [gains[k : k + 1, 0:1] for k in range(LEVELS)]

    def ratio(level):
        size, n, high = R[level], N[level], HIGH[level] // 128
        ref = levels[level - 1]
        strips = from_rows(rows, even_rows, odd_rows, level)
        for arr in range(2):
            store(full, arr, slice(0, size), load(ref, arr, slice(8, 8 + size)))
            for first, pair in zip((0, n), strips):
                for tile in range(W[level] // 128):
                    full[arr, tile, first : first + 8, :] += pair[arr][:, 128 * tile : 128 * tile + 128]
        for which, row, count, slot, place in PIECES:
            if which != level:
                continue
            one, two = even_cols[place : place + count, :], odd_cols[place : place + count, :]
            below = jnp.where(first_of_pair, two, one)
            above = jnp.where(first_of_pair, one, two)
            lane = lax.broadcasted_iota(jnp.int32, one.shape, 1)
            for arr in range(2):
                at = 8 * slot + 64 * arr
                low = jnp.where(lane < 3, roll(below, -at, 1), 0.0)
                up = n % 128
                up = jnp.where((lane >= up) & (lane < up + 3), roll(above, n - at, 1), 0.0)
                full[arr, 0, row : row + count, :] += low
                full[arr, high, row : row + count, :] += up
        mask = in_grid((size, W[level]), n, rows, cols)
        num, den = (load(full, arr, slice(0, size))[:, : W[level]] for arr in range(2))
        return mask, jnp.where(mask, num / jnp.where(mask, den, 1.0), 0.0)

    mask, value = ratio(LEVELS)
    piece = jnp.where(mask, -gain[LEVELS - 1] * value, 0.0)
    for level in range(LEVELS - 1, 0, -1):
        size, half = R[level], R[level] // 2
        tall[0 : R[level + 1], 0 : W[level]] = times(piece, wider[: W[level + 1], : W[level]])
        a, b, c = (tall[k : k + half, 0 : W[level]] for k in range(3))
        mask, value = ratio(level)
        even, odd = 0.5 * (a + b), 0.125 * (a + c) + 0.75 * b
        for tile in range(W[level] // 128):
            lanes = slice(128 * tile, 128 * tile + 128)
            wide[tile, pl.ds(0, half, stride=2), :] = even[:, lanes]
            wide[tile, pl.ds(1, half, stride=2), :] = odd[:, lanes]
        grown = jnp.concatenate([wide[tile, 0:size, :] for tile in range(W[level] // 128)], axis=1)
        change = gain[level] - gain[level - 1]
        piece = jnp.where(mask, change * value + grown, 0.0)
    tall[...] = times(piece, last[...])
    half = TILE // 2
    for tile in range(W[0] // 128):
        lanes = slice(128 * tile, 128 * tile + 128)
        a, b, c = (tall[k : k + half, lanes] for k in range(3))
        wide[tile, pl.ds(0, half, stride=2), :] = 0.125 * (a + c) + 0.75 * b
        wide[tile, pl.ds(1, half, stride=2), :] = 0.5 * (b + c)
        out[:, lanes] = gain[0] * shifted[:, lanes] + wide[tile, :, :]
    ones_expanded(rows, cols, last, field)


def end_vectors():
    low, high = np.ones(4 * N[LEVELS]), np.ones(4 * N[LEVELS])
    for _ in range(LEVELS):
        wide = [np.concatenate([[0.0], x, [1.0]]) for x in (low,)] + [np.concatenate([[1.0], high, [0.0]])]
        done = []
        for x in wide:
            a, b, c = x[:-2], x[1:-1], x[2:]
            done.append(np.stack([(a + 6 * b + c) / 8, (b + c) / 2], axis=1).reshape(-1))
        low, high = done
    return np.stack([low[:TILE], high[-TILE:]]).astype(np.float32)


def ones_expanded(rows, cols, last, field):
    ends = last[ENDS : ENDS + 16, :]

    def pick(place, count, order):
        kind = jnp.where(place == 0, 0, jnp.where(place == count - 1, 1, 2))
        k = lax.broadcasted_iota(jnp.int32, (16, 16), 0)
        source = lax.broadcasted_iota(jnp.int32, (16, 16), 1)
        hit = jnp.zeros((16, 16), jnp.bool_)
        for at, which in enumerate(order):
            hit = hit | ((k == at) & (source == 3 * kind + which))
        chosen = jnp.where(hit, 1.0, 0.0).astype(jnp.bfloat16)
        return jnp.dot(chosen, ends, preferred_element_type=jnp.float32).astype(jnp.bfloat16)

    a = pick(row_place(), rows, (0, 0, 1, 1, 0, 2))
    b = pick(lax.axis_index(COLS), cols, (0, 1, 0, 1, 2, 0))
    field[...] = lax.dot_general(a, b, (((0,), (0,)), ((), ())), preferred_element_type=jnp.float32)


def finish(rest, field, totals, out, done, sems):
    mean = totals[0:1, 0:1] / totals[0:1, 64:65]
    part = TILE // PARTS
    copies = []
    for k in range(PARTS):
        at = slice(k * part, k * part + part)
        done[at, :] = rest[at, :] + mean * field[at, :]
        copies.append(pltpu.make_async_copy(done.at[at], out.at[at], sems.at[k]))
        copies[-1].start()
    for copy in copies:
        copy.wait()


def swaps(count, first):
    return [p for i in range(first, count - 1, 2) for p in ((i, i + 1), (i + 1, i))]


def solution(mesh):
    rows, cols = mesh.shape["gy"] * mesh.shape["gz"], mesh.shape["gx"]
    wider = expand_matrix(W[2], W[1], 0)
    last = with_ends(expand_matrix(W[1], W[0], 1))
    f32 = jnp.float32
    anyw, vmem = pl.BlockSpec(memory_space=pltpu.HBM), pl.BlockSpec(memory_space=pltpu.VMEM)
    params = pltpu.CompilerParams(vmem_limit_bytes=VMEM)
    stored = [jax.ShapeDtypeStruct((2, W[level] // 128, A[level], 128), f32) for level in range(1, LEVELS + 1)]
    block = jax.ShapeDtypeStruct((SLOT, 128), f32)
    strip = jax.ShapeDtypeStruct((8, STRIPS), f32)
    small = jax.ShapeDtypeStruct((8, 128), f32)
    tile = jax.ShapeDtypeStruct((TILE, TILE), f32)

    def ring(axis, size, unit=1):
        def at(i, j):
            return [(i * unit + u, j * unit + u) for u in range(unit)]

        def both(pairs):
            return [p for i, j in pairs for p in at(i, j) + at(j, i)]

        rounds = []
        if size > 1:
            rounds.append(both([(i, i + 1) for i in range(0, size, 2)]))
        if size == 4:
            rounds.append(both([(0, 3), (1, 2)]))
        if size == 8:
            rounds.append(both([(0, 2), (1, 3), (4, 6), (5, 7)]))
            rounds.append(both([(i, 7 - i) for i in range(4)]))
        return [(axis, r) for r in rounds]

    def add(totals, rounds):
        for axis, pairs in rounds:
            totals = totals + lax.ppermute(totals, axis, pairs)
        return totals

    gy, gz, gx = ring("gy", mesh.shape["gy"]), ring("gz", mesh.shape["gz"]), ring(COLS, cols // 2, 2)

    def local(heights, ids, offset, weight, gain):
        def row(x):
            return jnp.pad(x, (0, 128 - x.shape[0]))[None]

        tables = jnp.concatenate([row(offset), row(weight), row(gain), jnp.zeros((5, 128), f32)], axis=0)
        shifted, *rest = pl.pallas_call(
            lambda *refs: pyramid(rows, cols, *refs),
            out_shape=[tile, *stored, block, block, strip, strip, small, small],
            in_specs=[anyw] * 3,
            out_specs=[vmem] * 13,
            scratch_shapes=[
                pltpu.VMEM((2, W[0] // 128, A[0], 128), f32),
                pltpu.VMEM((TILE, TILE), f32),
                pltpu.VMEM((TILE, TILE), jnp.int32),
                pltpu.VMEM((W[0], W[1]), jnp.bfloat16),
                pltpu.VMEM((W[1], W[2]), jnp.bfloat16),
                pltpu.SMEM((8, 128), f32),
                pltpu.SemaphoreType.DMA((1 + 2 * PARTS,)),
            ],
            compiler_params=pltpu.CompilerParams(vmem_limit_bytes=FIRST_VMEM),
            name="pyramid",
        )(heights, ids, tables)
        levels, (low, high, even_rows, odd_rows, totals, gains) = rest[:LEVELS], rest[LEVELS:]
        even_rows = lax.ppermute(even_rows, ROWS, swaps(rows, 0))
        odd_rows = lax.ppermute(odd_rows, ROWS, swaps(rows, 1) + [(0, rows - 1), (rows - 1, 0)])
        totals = add(totals + even_rows[:, STRIPS - 128 :], gz[1:])
        even_cols, odd_cols = pl.pallas_call(
            lambda *refs: edges(rows, *refs),
            out_shape=[jax.ShapeDtypeStruct((SLOT + 8, 128), f32)] * 2,
            in_specs=[vmem] * 5,
            out_specs=[vmem] * 2,
            scratch_shapes=[pltpu.VMEM((SLOT, 128), f32)] * 2,
            compiler_params=params,
            name="edges",
        )(low, high, even_rows, odd_rows, totals)
        even_cols = lax.ppermute(even_cols, COLS, swaps(cols, 0))
        odd_cols = lax.ppermute(odd_cols, COLS, swaps(cols, 1))
        totals = add(totals + even_cols[SLOT:], gx[:2] + gy + gx[2:])
        rest, field = pl.pallas_call(
            lambda *refs: collapse(rows, cols, *refs),
            out_shape=[tile, tile],
            in_specs=[vmem] * 14,
            out_specs=[vmem] * 2,
            scratch_shapes=[pltpu.VMEM((R[1], TILE), f32), pltpu.VMEM((W[0] // 128, TILE, 128), f32)]
            + [pltpu.VMEM((2, W[1] // 128, R[1], 128), f32)],
            compiler_params=params,
            name="collapse",
        )(gains, *levels, even_rows, odd_rows, even_cols, odd_cols, wider, last, shifted)
        return pl.pallas_call(
            finish,
            out_shape=tile,
            in_specs=[vmem] * 3,
            out_specs=pl.BlockSpec(memory_space=pl.ANY),
            scratch_shapes=[pltpu.VMEM((TILE, TILE), f32), pltpu.SemaphoreType.DMA((PARTS,))],
            compiler_params=params,
            name="finish",
        )(rest, field, totals)

    spec = P(ROWS, COLS)
    return jax.shard_map(
        local, mesh=mesh, in_specs=(spec, spec, P(), P(), P()), out_specs=spec, check_vma=False
    )
```

```python
import jax
import jax.numpy as jnp
import numpy as np
from jax import lax
from jax.experimental import pallas as pl
from jax.experimental.pallas import tpu as pltpu
from jax.sharding import PartitionSpec as P

SCENES = 16
LEVELS = 6
TILE = 512
KERN = (0.0625, 0.25, 0.375, 0.25, 0.0625)
ROWS = ("gy", "gz")
COLS = "gx"

N = [TILE >> level for level in range(LEVELS + 1)]
R = [0, 272, 144, 80, 48, 32, 32]
A = [560, 304, 176, 112, 80, 80, 40]
W = [512, 384, 256, 128, 128, 128, 128]
STRIP = [0, 0, 384, 640, 768, 896, 1024]
STRIPS = 1152
SLOT = 80
PIECES = [
    (1, 0, 80, 0, 0),
    (1, 80, 80, 1, 0),
    (1, 160, 80, 2, 0),
    (1, 240, 32, 3, 0),
    (6, 0, 32, 3, 32),
    (2, 0, 80, 4, 0),
    (2, 80, 64, 5, 0),
    (3, 0, 80, 6, 0),
    (4, 0, 48, 7, 0),
    (5, 0, 32, 7, 48),
]
HIGH = [0, 256, 128, 0, 0, 0, 0]
TURN = [0, 0, 0, 64, 96, 112, 120]
PARTS = 4
VMEM = 40 * 1024 * 1024
FIRST_VMEM = 50 * 1024 * 1024


def reduce_matrix(rows, cols, shift):
    t = lax.broadcasted_iota(jnp.int32, (rows, cols), 0)
    s = lax.broadcasted_iota(jnp.int32, (rows, cols), 1)
    d = jnp.abs(t - 2 * s + shift)
    out = jnp.where(d == 2, KERN[0], 0.0)
    return jnp.where(d == 1, KERN[1], jnp.where(d == 0, KERN[2], out)).astype(jnp.bfloat16)


def expand_matrix(rows, cols, shift):
    out = np.zeros((rows, cols), np.float32)
    for c in range(cols):
        s = c + shift
        j = s // 2
        taps = ((j, 0.5), (j + 1, 0.5)) if s % 2 == 0 else ((j, 0.125), (j + 1, 0.75), (j + 2, 0.125))
        for t, value in taps:
            if 0 <= t < rows:
                out[t, c] = value
    return out.astype(jnp.bfloat16)


def times(x, matrix):
    hi = x.astype(jnp.bfloat16)
    rest = x - hi.astype(jnp.float32)
    mid = rest.astype(jnp.bfloat16)
    lo = (rest - mid.astype(jnp.float32)).astype(jnp.bfloat16)
    out = jnp.dot(hi, matrix, preferred_element_type=jnp.float32)
    out = out + jnp.dot(mid, matrix, preferred_element_type=jnp.float32)
    return out + jnp.dot(lo, matrix, preferred_element_type=jnp.float32)


def load(ref, arr, at):
    return jnp.concatenate([ref[arr, tile, at, :] for tile in range(ref.shape[1])], axis=1)


def store(ref, arr, at, value):
    for tile in range(value.shape[1] // 128):
        ref[arr, tile, at, :] = value[:, 128 * tile : 128 * tile + 128]


def row_place():
    return lax.axis_index("gy") * lax.axis_size("gz") + lax.axis_index("gz")


def in_grid(shape, n, rows, cols):
    def side(dim, place, count):
        s = lax.broadcasted_iota(jnp.int32, shape, dim)
        low = jnp.where(place == 0, 1, 0)
        high = jnp.where(place == count - 1, n, n + 2)
        return (s >= low) & (s <= high)

    return side(0, row_place(), rows) & side(1, lax.axis_index(COLS), cols)


def roll(x, shift, axis):
    return pltpu.roll(x, shift % x.shape[axis], axis) if shift % x.shape[axis] else x


def three(num, den, low_slot):
    lane = lax.broadcasted_iota(jnp.int32, num.shape, 1)
    at = 8 * low_slot
    num = jnp.where((lane >= at) & (lane < at + 3), roll(num, at, 1), 0.0)
    return jnp.where((lane >= at + 64) & (lane < at + 67), roll(den, at + 64, 1), num)


def ones_expanded(place, count, tall, wide):
    for level in range(LEVELS, 0, -1):
        s = lax.broadcasted_iota(jnp.int32, (R[level], 128), 0)
        inside = (s >= jnp.where(place == 0, 1, 0)) & (s <= jnp.where(place == count - 1, N[level], N[level] + 2))
        x = 1.0 if level == LEVELS else wide[0 : R[level], :]
        tall[0 : R[level], :] = jnp.where(inside, x, 0.0)
        half = R[level - 1] // 2 if level > 1 else TILE // 2
        a, b, c = (tall[k : k + half, :] for k in range(3))
        even, odd = 0.5 * (a + b), 0.125 * (a + c) + 0.75 * b
        if level == 1:
            even, odd = odd, 0.5 * (b + c)
        wide[pl.ds(0, half, stride=2), :] = even
        wide[pl.ds(1, half, stride=2), :] = odd


def scenes(rows, cols, heights_in, ids_in, tables, *refs):
    base, (shifted, totals, gains, ups, downs, heights, ids, tall, wide, table, sems) = refs[:8], refs[8:]
    step, part = 32, TILE // PARTS
    pairs = [(tables, table)]
    for k in range(PARTS):
        at = slice(k * part, k * part + part)
        pairs.append((heights_in.at[at], heights.at[at]))
        pairs.append((ids_in.at[at], ids.at[at]))
    copies = [pltpu.make_async_copy(a, b, sems.at[k]) for k, (a, b) in enumerate(pairs)]
    for copy in copies:
        copy.start()
    for ref in base:
        ref[0:8, :] = jnp.zeros((8, 128), jnp.float32)
        ref[8 + TILE :, :] = jnp.zeros((A[0] - 8 - TILE, 128), jnp.float32)
    ones_expanded(lax.axis_index(COLS), cols, tall, wide)
    for tile in range(4):
        downs[:, 128 * tile : 128 * tile + 128] = wide[128 * tile : 128 * tile + 128, :].T[0:8, :]
    ones_expanded(row_place(), rows, tall, wide)
    ups[...] = wide[...]

    def cells(i, sums):
        at = pl.ds(pl.multiple_of(i * step, step), step)
        to = pl.ds(pl.multiple_of(i * step + 8, 8), step)
        which = ids[at, :]
        bits = [(which & (1 << b)) != 0 for b in range(4)]

        def lookup(first):
            values = [table[first + s] for s in range(SCENES)]
            for b in range(4):
                values = [
                    jnp.where(bits[b], values[2 * k + 1], values[2 * k]) for k in range(len(values) // 2)
                ]
            return values[0]

        w = lookup(SCENES)
        h = heights[at, :] + lookup(0)
        shifted[at, :] = h
        up = ups[at, :]
        up = jnp.concatenate([up] * (W[0] // 128), axis=1)
        out = []
        for arr, value in enumerate((w * h, w)):
            for tile in range(W[0] // 128):
                base[4 * arr + tile][to, :] = value[:, 128 * tile : 128 * tile + 128]
            value = value * up
            out.append(sums[arr] + sum(value[8 * k : 8 * k + 8] for k in range(step // 8)))
        return tuple(out)

    copies[0].wait()
    sums = (jnp.zeros((8, TILE), jnp.float32),) * 2
    for k in range(PARTS):
        copies[1 + 2 * k].wait()
        copies[2 + 2 * k].wait()
        sums = lax.fori_loop(k * part // step, (k + 1) * part // step, cells, sums)
    sums = [jnp.sum(x * downs[...]) for x in sums]
    lane = lax.broadcasted_iota(jnp.int32, (8, 128), 1)
    sub = lax.broadcasted_iota(jnp.int32, (8, 128), 0)
    totals[...] = jnp.where(lane < 64, sums[0], sums[1])
    gains[...] = sum(jnp.where(sub == k, table[2 * SCENES + k], 0.0) for k in range(LEVELS))


def pyramid(rows, cols, *refs):
    base, refs = refs[:8], refs[8:]
    levels, (even_rows, odd_rows, first, later) = refs[:LEVELS], refs[LEVELS:]
    first[...] = reduce_matrix(W[0], W[1], 2)
    later[...] = reduce_matrix(W[1], W[2], 1)
    for level in range(1, LEVELS + 1):
        target = levels[level - 1]
        start = 4 if level == 1 else 5
        size = R[level]
        matrix = first[...] if level == 1 else later[: W[level - 1], : W[level]]
        mask = in_grid((size, W[level]), N[level], rows, cols)
        for arr in range(2):
            places = [pl.ds(start + k, size, stride=2) for k in range(5)]
            if level == 1:
                taps = [jnp.concatenate([base[4 * arr + t][at, :] for t in range(4)], axis=1) for at in places]
            else:
                taps = [load(levels[level - 2], arr, at) for at in places]
            tall = KERN[0] * (taps[0] + taps[4]) + KERN[1] * (taps[1] + taps[3]) + KERN[2] * taps[2]
            part = jnp.where(mask, times(tall, matrix), 0.0)
            store(target, arr, slice(0, 8), jnp.zeros((8, W[level]), jnp.float32))
            store(target, arr, slice(8, 8 + size), part)
            if A[level] > 8 + size:
                rest = A[level] - 8 - size
                store(target, arr, slice(8 + size, A[level]), jnp.zeros((rest, W[level]), jnp.float32))

    even = row_place() % 2 == 0
    def strips(level, at):
        ref = levels[level - 1]
        num = load(ref, 0, slice(at, at + 8))
        den = pltpu.roll(load(ref, 1, slice(at, at + 8)), 4, 0)
        sub = lax.broadcasted_iota(jnp.int32, num.shape, 0)
        return jnp.where(sub < 3, num, jnp.where((sub > 3) & (sub < 7), den, 0.0))

    for level in range(1, LEVELS + 1):
        low, high = strips(level, 8), strips(level, 8 + N[level])
        to = slice(STRIP[level], STRIP[level] + W[level])
        even_rows[:, to] = jnp.where(even, high, low)
        odd_rows[:, to] = jnp.where(even, low, high)


def pack(*refs):
    levels, (low_cols, high_cols) = refs[:LEVELS], refs[LEVELS:]
    low_cols[...] = jnp.zeros(low_cols.shape, jnp.float32)
    high_cols[...] = jnp.zeros(high_cols.shape, jnp.float32)
    for level, row, size, slot, place in PIECES:
        tile, turn = HIGH[level] // 128, TURN[level]
        num, den = levels[level - 1].at[0], levels[level - 1].at[1]
        at, to = slice(8 + row, 8 + row + size), slice(place, place + size)
        low_cols[to, :] += three(num[0, at, :], den[0, at, :], slot)
        high_cols[to, :] += three(roll(num[tile, at, :], turn, 1), roll(den[tile, at, :], turn, 1), slot)


def from_rows(rows, even_rows, odd_rows, level):
    even = row_place() % 2 == 0
    to = slice(STRIP[level], STRIP[level] + W[level])
    one, two = even_rows[:, to], odd_rows[:, to]
    near = lax.broadcasted_iota(jnp.int32, one.shape, 0) < 3
    out = []
    row = row_place()
    above = (jnp.where(even, two, one), row > 0)
    below = (jnp.where(even, one, two), row < rows - 1)
    for got, there in (above, below):
        keep = near & there
        out.append((jnp.where(keep, got, 0.0), jnp.where(keep, pltpu.roll(got, 4, 0), 0.0)))
    return out


def edges(rows, low_in, high_in, even_rows, odd_rows, totals, even_cols, odd_cols, low, high):
    low[...] = low_in[...]
    high[...] = high_in[...]
    for level in range(1, LEVELS + 1):
        tile, turn = HIGH[level], TURN[level]
        for at, (num, den) in zip((0, N[level]), from_rows(rows, even_rows, odd_rows, level)):
            for which, row, size, slot, place in PIECES:
                if which == level and row <= at < row + size:
                    to = slice(place + at - row, place + at - row + 8)
                    low[to, :] += three(num[:, 0:128], den[:, 0:128], slot)
                    num, den = (roll(x[:, tile : tile + 128], turn, 1) for x in (num, den))
                    high[to, :] += three(num, den, slot)
    even = lax.axis_index(COLS) % 2 == 0
    one, two = low[...], high[...]
    even_cols[0:SLOT, :] = jnp.where(even, two, one)
    odd_cols[0:SLOT, :] = jnp.where(even, one, two)
    even_cols[SLOT:, :] = totals[...]
    odd_cols[SLOT:, :] = totals[...]


def collapse(rows, cols, gains, l1, l2, l3, l4, l5, l6, even_rows, odd_rows, even_cols, odd_cols, wider, last, shifted, out, tall, wide, full):
    levels = (l1, l2, l3, l4, l5, l6)
    first_of_pair = lax.axis_index(COLS) % 2 == 0
    gain = [gains[k : k + 1, 0:1] for k in range(LEVELS)]

    def ratio(level):
        size, n, high = R[level], N[level], HIGH[level] // 128
        ref = levels[level - 1]
        strips = from_rows(rows, even_rows, odd_rows, level)
        for arr in range(2):
            store(full, arr, slice(0, size), load(ref, arr, slice(8, 8 + size)))
            for first, pair in zip((0, n), strips):
                for tile in range(W[level] // 128):
                    full[arr, tile, first : first + 8, :] += pair[arr][:, 128 * tile : 128 * tile + 128]
        for which, row, count, slot, place in PIECES:
            if which != level:
                continue
            one, two = even_cols[place : place + count, :], odd_cols[place : place + count, :]
            below = jnp.where(first_of_pair, two, one)
            above = jnp.where(first_of_pair, one, two)
            lane = lax.broadcasted_iota(jnp.int32, one.shape, 1)
            for arr in range(2):
                at = 8 * slot + 64 * arr
                low = jnp.where(lane < 3, roll(below, -at, 1), 0.0)
                up = n % 128
                up = jnp.where((lane >= up) & (lane < up + 3), roll(above, n - at, 1), 0.0)
                full[arr, 0, row : row + count, :] += low
                full[arr, high, row : row + count, :] += up
        mask = in_grid((size, W[level]), n, rows, cols)
        num, den = (load(full, arr, slice(0, size))[:, : W[level]] for arr in range(2))
        return mask, jnp.where(mask, num / jnp.where(mask, den, 1.0), 0.0)

    mask, value = ratio(LEVELS)
    piece = jnp.where(mask, -gain[LEVELS - 1] * value, 0.0)
    for level in range(LEVELS - 1, 0, -1):
        size, half = R[level], R[level] // 2
        tall[0 : R[level + 1], 0 : W[level]] = times(piece, wider[: W[level + 1], : W[level]])
        a, b, c = (tall[k : k + half, 0 : W[level]] for k in range(3))
        mask, value = ratio(level)
        even, odd = 0.5 * (a + b), 0.125 * (a + c) + 0.75 * b
        for tile in range(W[level] // 128):
            lanes = slice(128 * tile, 128 * tile + 128)
            wide[tile, pl.ds(0, half, stride=2), :] = even[:, lanes]
            wide[tile, pl.ds(1, half, stride=2), :] = odd[:, lanes]
        grown = jnp.concatenate([wide[tile, 0:size, :] for tile in range(W[level] // 128)], axis=1)
        change = gain[level] - gain[level - 1]
        piece = jnp.where(mask, change * value + grown, 0.0)
    tall[...] = times(piece, last[...])
    half = TILE // 2
    for tile in range(W[0] // 128):
        lanes = slice(128 * tile, 128 * tile + 128)
        a, b, c = (tall[k : k + half, lanes] for k in range(3))
        wide[tile, pl.ds(0, half, stride=2), :] = 0.125 * (a + c) + 0.75 * b
        wide[tile, pl.ds(1, half, stride=2), :] = 0.5 * (b + c)
        out[:, lanes] = gain[0] * shifted[:, lanes] + wide[tile, :, :]


def finish(rest, ups, downs, totals, out, done, sems):
    mean = totals[0:1, 0:1] / totals[0:1, 64:65]
    part = TILE // PARTS
    copies = []
    for k in range(PARTS):
        at = slice(k * part, k * part + part)
        up = mean * ups[at, :]
        for tile in range(W[0] // 128):
            lanes = slice(128 * tile, 128 * tile + 128)
            done[at, lanes] = rest[at, lanes] + up * downs[0:1, lanes]
        copies.append(pltpu.make_async_copy(done.at[at], out.at[at], sems.at[k]))
        copies[-1].start()
    for copy in copies:
        copy.wait()


def swaps(count, first):
    return [p for i in range(first, count - 1, 2) for p in ((i, i + 1), (i + 1, i))]


def solution(mesh):
    rows, cols = mesh.shape["gy"] * mesh.shape["gz"], mesh.shape["gx"]
    wider = expand_matrix(W[2], W[1], 0)
    last = expand_matrix(W[1], W[0], 1)
    f32 = jnp.float32
    anyw, vmem = pl.BlockSpec(memory_space=pltpu.HBM), pl.BlockSpec(memory_space=pltpu.VMEM)
    params = pltpu.CompilerParams(vmem_limit_bytes=VMEM)
    stored = [jax.ShapeDtypeStruct((2, W[level] // 128, A[level], 128), f32) for level in range(1, LEVELS + 1)]
    block = jax.ShapeDtypeStruct((SLOT, 128), f32)
    strip = jax.ShapeDtypeStruct((8, STRIPS), f32)
    small = jax.ShapeDtypeStruct((8, 128), f32)
    tile = jax.ShapeDtypeStruct((TILE, TILE), f32)

    def ring(axis, size, unit=1):
        def at(i, j):
            return [(i * unit + u, j * unit + u) for u in range(unit)]

        def both(pairs):
            return [p for i, j in pairs for p in at(i, j) + at(j, i)]

        rounds = []
        if size > 1:
            rounds.append(both([(i, i + 1) for i in range(0, size, 2)]))
        if size == 4:
            rounds.append(both([(0, 3), (1, 2)]))
        if size == 8:
            rounds.append(both([(0, 2), (1, 3), (4, 6), (5, 7)]))
            rounds.append(both([(i, 7 - i) for i in range(4)]))
        return [(axis, r) for r in rounds]

    def add(totals, rounds):
        for axis, pairs in rounds:
            totals = totals + lax.ppermute(totals, axis, pairs)
        return totals

    gy, gz, gx = ring("gy", mesh.shape["gy"]), ring("gz", mesh.shape["gz"]), ring(COLS, cols // 2, 2)

    def local(heights, ids, offset, weight, gain):
        tables = jnp.concatenate([offset, weight, gain])
        *base, shifted, totals, gains, ups, downs = pl.pallas_call(
            lambda *refs: scenes(rows, cols, *refs),
            out_shape=[jax.ShapeDtypeStruct((A[0], 128), f32)] * 8
            + [tile, small, small, jax.ShapeDtypeStruct((TILE, 128), f32), jax.ShapeDtypeStruct((8, TILE), f32)],
            in_specs=[anyw] * 3,
            out_specs=[vmem] * 13,
            scratch_shapes=[
                pltpu.VMEM((TILE, TILE), f32),
                pltpu.VMEM((TILE, TILE), jnp.int32),
                pltpu.VMEM((R[1], 128), f32),
                pltpu.VMEM((TILE, 128), f32),
                pltpu.SMEM((2 * SCENES + LEVELS,), f32),
                pltpu.SemaphoreType.DMA((1 + 2 * PARTS,)),
            ],
            compiler_params=pltpu.CompilerParams(vmem_limit_bytes=FIRST_VMEM),
            name="scenes",
        )(heights, ids, tables)
        totals = add(totals, gz[1:])
        *levels, even_rows, odd_rows = pl.pallas_call(
            lambda *refs: pyramid(rows, cols, *refs),
            out_shape=[*stored, strip, strip],
            in_specs=[vmem] * 8,
            out_specs=[vmem] * (LEVELS + 2),
            scratch_shapes=[
                pltpu.VMEM((W[0], W[1]), jnp.bfloat16),
                pltpu.VMEM((W[1], W[2]), jnp.bfloat16),
            ],
            compiler_params=params,
            name="pyramid",
        )(*base)
        low, high = pl.pallas_call(
            pack,
            out_shape=[block, block],
            in_specs=[vmem] * LEVELS,
            out_specs=[vmem] * 2,
            compiler_params=params,
            name="pack",
        )(*levels)
        even_rows = jnp.concatenate([even_rows, totals], axis=1)
        even_rows = lax.ppermute(even_rows, ROWS, swaps(rows, 0))
        odd_rows = lax.ppermute(odd_rows, ROWS, swaps(rows, 1) + [(0, rows - 1), (rows - 1, 0)])
        totals = add(totals + even_rows[:, STRIPS:], gy[:1])
        even_cols, odd_cols = pl.pallas_call(
            lambda *refs: edges(rows, *refs),
            out_shape=[jax.ShapeDtypeStruct((SLOT + 8, 128), f32)] * 2,
            in_specs=[vmem] * 5,
            out_specs=[vmem] * 2,
            scratch_shapes=[pltpu.VMEM((SLOT, 128), f32)] * 2,
            compiler_params=params,
            name="edges",
        )(low, high, even_rows, odd_rows, totals)
        even_cols = lax.ppermute(even_cols, COLS, swaps(cols, 0))
        odd_cols = lax.ppermute(odd_cols, COLS, swaps(cols, 1))
        totals = add(totals + even_cols[SLOT:], gy[1:] + gx[:2])
        rest = pl.pallas_call(
            lambda *refs: collapse(rows, cols, *refs),
            out_shape=tile,
            in_specs=[vmem] * 14,
            out_specs=vmem,
            scratch_shapes=[pltpu.VMEM((R[1], TILE), f32), pltpu.VMEM((W[0] // 128, TILE, 128), f32)]
            + [pltpu.VMEM((2, W[1] // 128, R[1], 128), f32)],
            compiler_params=params,
            name="collapse",
        )(gains, *levels, even_rows, odd_rows, even_cols, odd_cols, wider, last, shifted)
        totals, rest = lax.optimization_barrier((totals, rest))
        totals = add(totals, gx[2:])
        return pl.pallas_call(
            finish,
            out_shape=tile,
            in_specs=[vmem] * 4,
            out_specs=pl.BlockSpec(memory_space=pl.ANY),
            scratch_shapes=[pltpu.VMEM((TILE, TILE), f32), pltpu.SemaphoreType.DMA((PARTS,))],
            compiler_params=params,
            name="finish",
        )(rest, ups, downs, totals)

    spec = P(ROWS, COLS)
    return jax.shard_map(
        local, mesh=mesh, in_specs=(spec, spec, P(), P(), P()), out_specs=spec, check_vma=False
    )
```

```python
import jax
import jax.numpy as jnp
import numpy as np
from jax import lax
from jax.experimental import pallas as pl
from jax.experimental.pallas import tpu as pltpu
from jax.sharding import PartitionSpec as P

SCENES = 16
LEVELS = 6
TILE = 512
KERN = (0.0625, 0.25, 0.375, 0.25, 0.0625)
ROWS = ("gy", "gz")
COLS = "gx"

N = [TILE >> level for level in range(LEVELS + 1)]
R = [0, 272, 144, 80, 48, 32, 32]
A = [560, 304, 176, 112, 80, 80, 40]
W = [512, 384, 256, 128, 128, 128, 128]
STRIP = [0, 0, 384, 640, 768, 896, 1024]
STRIPS = 1152
SLOT = 80
PIECES = [
    (1, 0, 80, 0, 0),
    (1, 80, 80, 1, 0),
    (1, 160, 80, 2, 0),
    (1, 240, 32, 3, 0),
    (6, 0, 32, 3, 32),
    (2, 0, 80, 4, 0),
    (2, 80, 64, 5, 0),
    (3, 0, 80, 6, 0),
    (4, 0, 48, 7, 0),
    (5, 0, 32, 7, 48),
]
HIGH = [0, 256, 128, 0, 0, 0, 0]
TURN = [0, 0, 0, 64, 96, 112, 120]
PARTS = 4
BIG = 11
VMEM = 40 * 1024 * 1024
FIRST_VMEM = 50 * 1024 * 1024


def reduce_matrix(rows, cols, shift):
    t = lax.broadcasted_iota(jnp.int32, (rows, cols), 0)
    s = lax.broadcasted_iota(jnp.int32, (rows, cols), 1)
    d = jnp.abs(t - 2 * s + shift)
    out = jnp.where(d == 2, KERN[0], 0.0)
    return jnp.where(d == 1, KERN[1], jnp.where(d == 0, KERN[2], out)).astype(jnp.bfloat16)


def expand_matrix(rows, cols, shift):
    out = np.zeros((rows, cols), np.float32)
    for c in range(cols):
        s = c + shift
        j = s // 2
        taps = ((j, 0.5), (j + 1, 0.5)) if s % 2 == 0 else ((j, 0.125), (j + 1, 0.75), (j + 2, 0.125))
        for t, value in taps:
            if 0 <= t < rows:
                out[t, c] = value
    return out.astype(jnp.bfloat16)


def times(x, matrix):
    hi = x.astype(jnp.bfloat16)
    rest = x - hi.astype(jnp.float32)
    mid = rest.astype(jnp.bfloat16)
    lo = (rest - mid.astype(jnp.float32)).astype(jnp.bfloat16)
    out = jnp.dot(hi, matrix, preferred_element_type=jnp.float32)
    out = out + jnp.dot(mid, matrix, preferred_element_type=jnp.float32)
    return out + jnp.dot(lo, matrix, preferred_element_type=jnp.float32)


def load(ref, arr, at):
    return jnp.concatenate([ref[arr, tile, at, :] for tile in range(ref.shape[1])], axis=1)


def store(ref, arr, at, value):
    for tile in range(value.shape[1] // 128):
        ref[arr, tile, at, :] = value[:, 128 * tile : 128 * tile + 128]


def row_place():
    return lax.axis_index("gy") * lax.axis_size("gz") + lax.axis_index("gz")


def in_grid(shape, n, rows, cols):
    def side(dim, place, count):
        s = lax.broadcasted_iota(jnp.int32, shape, dim)
        low = jnp.where(place == 0, 1, 0)
        high = jnp.where(place == count - 1, n, n + 2)
        return (s >= low) & (s <= high)

    return side(0, row_place(), rows) & side(1, lax.axis_index(COLS), cols)


def roll(x, shift, axis):
    return pltpu.roll(x, shift % x.shape[axis], axis) if shift % x.shape[axis] else x


def three(num, den, low_slot):
    lane = lax.broadcasted_iota(jnp.int32, num.shape, 1)
    at = 8 * low_slot
    num = jnp.where((lane >= at) & (lane < at + 3), roll(num, at, 1), 0.0)
    return jnp.where((lane >= at + 64) & (lane < at + 67), roll(den, at + 64, 1), num)


def ones_expanded(place, count, tall, wide):
    for level in range(LEVELS, 0, -1):
        s = lax.broadcasted_iota(jnp.int32, (R[level], 128), 0)
        inside = (s >= jnp.where(place == 0, 1, 0)) & (s <= jnp.where(place == count - 1, N[level], N[level] + 2))
        x = 1.0 if level == LEVELS else wide[0 : R[level], :]
        tall[0 : R[level], :] = jnp.where(inside, x, 0.0)
        half = R[level - 1] // 2 if level > 1 else TILE // 2
        a, b, c = (tall[k : k + half, :] for k in range(3))
        even, odd = 0.5 * (a + b), 0.125 * (a + c) + 0.75 * b
        if level == 1:
            even, odd = odd, 0.5 * (b + c)
        wide[pl.ds(0, half, stride=2), :] = even
        wide[pl.ds(1, half, stride=2), :] = odd


def scenes(rows, cols, heights_in, ids_in, tables, *refs):
    base, (shifted, totals, gains, ups, downs, heights, ids, tall, wide, table, sems) = refs[:8], refs[8:]
    step, part = 32, TILE // PARTS
    pairs = [(tables, table)]
    for k in range(PARTS):
        at = slice(k * part, k * part + part)
        pairs.append((heights_in.at[at], heights.at[at]))
        pairs.append((ids_in.at[at], ids.at[at]))
    copies = [pltpu.make_async_copy(a, b, sems.at[k]) for k, (a, b) in enumerate(pairs)]
    for copy in copies:
        copy.start()
    for ref in base:
        ref[0:8, :] = jnp.zeros((8, 128), jnp.float32)
        ref[8 + TILE :, :] = jnp.zeros((A[0] - 8 - TILE, 128), jnp.float32)
    ones_expanded(lax.axis_index(COLS), cols, tall, wide)
    for tile in range(4):
        downs[:, 128 * tile : 128 * tile + 128] = wide[128 * tile : 128 * tile + 128, :].T[0:8, :]
    ones_expanded(row_place(), rows, tall, wide)
    ups[...] = wide[...]

    def cells(i, sums):
        at = pl.ds(pl.multiple_of(i * step, step), step)
        to = pl.ds(pl.multiple_of(i * step + 8, 8), step)
        which = ids[at, :]
        bits = [(which & (1 << b)) != 0 for b in range(4)]

        def lookup(first):
            values = [table[first + s] for s in range(SCENES)]
            for b in range(4):
                values = [
                    jnp.where(bits[b], values[2 * k + 1], values[2 * k]) for k in range(len(values) // 2)
                ]
            return values[0]

        tiles = [which[:, 128 * t : 128 * t + 128] for t in range(W[0] // 128)]
        tiles = [jnp.take_along_axis(weights, t, axis=1, mode="promise_in_bounds") for t in tiles]
        w = jnp.concatenate(tiles, axis=1)
        h = heights[at, :] + lookup(0)
        shifted[at, :] = h
        up = ups[at, :]
        up = jnp.concatenate([up] * (W[0] // 128), axis=1)
        out = []
        for arr, value in enumerate((w * h, w)):
            for tile in range(W[0] // 128):
                base[4 * arr + tile][to, :] = value[:, 128 * tile : 128 * tile + 128]
            value = value * up
            out.append(sums[arr] + sum(value[8 * k : 8 * k + 8] for k in range(step // 8)))
        return tuple(out)

    copies[0].wait()
    lane = lax.broadcasted_iota(jnp.int32, (step, 128), 1)
    weights = jnp.zeros((step, 128), jnp.float32)
    for s in range(SCENES):
        weights = jnp.where(lane == s, table[SCENES + s], weights)
    sums = (jnp.zeros((8, TILE), jnp.float32),) * 2
    for k in range(PARTS):
        copies[1 + 2 * k].wait()
        copies[2 + 2 * k].wait()
        sums = lax.fori_loop(k * part // step, (k + 1) * part // step, cells, sums)
    sums = [jnp.sum(x * downs[...]) for x in sums]
    lane = lax.broadcasted_iota(jnp.int32, (8, 128), 1)
    sub = lax.broadcasted_iota(jnp.int32, (8, 128), 0)
    totals[...] = jnp.where(lane < 64, sums[0], sums[1])
    gains[...] = sum(jnp.where(sub == k, table[2 * SCENES + k], 0.0) for k in range(LEVELS))


def pyramid(rows, cols, *refs):
    base, refs = refs[:8], refs[8:]
    levels, (even_rows, odd_rows, first, later) = refs[:LEVELS], refs[LEVELS:]
    first[...] = reduce_matrix(W[0], W[1], 2)
    later[...] = reduce_matrix(W[1], W[2], 1)
    for level in range(1, LEVELS + 1):
        target = levels[level - 1]
        start = 4 if level == 1 else 5
        size = R[level]
        matrix = first[...] if level == 1 else later[: W[level - 1], : W[level]]
        mask = in_grid((size, W[level]), N[level], rows, cols)
        for arr in range(2):
            places = [pl.ds(start + k, size, stride=2) for k in range(5)]
            if level == 1:
                taps = [jnp.concatenate([base[4 * arr + t][at, :] for t in range(4)], axis=1) for at in places]
            else:
                taps = [load(levels[level - 2], arr, at) for at in places]
            tall = KERN[0] * (taps[0] + taps[4]) + KERN[1] * (taps[1] + taps[3]) + KERN[2] * taps[2]
            if level == 1:
                part = [times(tall, matrix[:, 0:256]), times(tall[:, 384:512], matrix[384:512, 256:384])]
                part = jnp.concatenate(part, axis=1)
            else:
                part = times(tall, matrix)
            part = jnp.where(mask, part, 0.0)
            store(target, arr, slice(0, 8), jnp.zeros((8, W[level]), jnp.float32))
            store(target, arr, slice(8, 8 + size), part)
            if A[level] > 8 + size:
                rest = A[level] - 8 - size
                store(target, arr, slice(8 + size, A[level]), jnp.zeros((rest, W[level]), jnp.float32))

    even = row_place() % 2 == 0
    def strips(level, at):
        ref = levels[level - 1]
        num = load(ref, 0, slice(at, at + 8))
        den = pltpu.roll(load(ref, 1, slice(at, at + 8)), 4, 0)
        sub = lax.broadcasted_iota(jnp.int32, num.shape, 0)
        return jnp.where(sub < 3, num, jnp.where((sub > 3) & (sub < 7), den, 0.0))

    for level in range(1, LEVELS + 1):
        low, high = strips(level, 8), strips(level, 8 + N[level])
        to = slice(STRIP[level], STRIP[level] + W[level])
        even_rows[:, to] = jnp.where(even, high, low)
        odd_rows[:, to] = jnp.where(even, low, high)


def pack(*refs):
    levels, (low_cols, high_cols) = refs[:LEVELS], refs[LEVELS:]
    low_cols[...] = jnp.zeros(low_cols.shape, jnp.float32)
    high_cols[...] = jnp.zeros(high_cols.shape, jnp.float32)
    for level, row, size, slot, place in PIECES:
        tile, turn = HIGH[level] // 128, TURN[level]
        num, den = levels[level - 1].at[0], levels[level - 1].at[1]
        at, to = slice(8 + row, 8 + row + size), slice(place, place + size)
        low_cols[to, :] += three(num[0, at, :], den[0, at, :], slot)
        high_cols[to, :] += three(roll(num[tile, at, :], turn, 1), roll(den[tile, at, :], turn, 1), slot)


def from_rows(rows, even_rows, odd_rows, level):
    even = row_place() % 2 == 0
    to = slice(STRIP[level], STRIP[level] + W[level])
    one, two = even_rows[:, to], odd_rows[:, to]
    near = lax.broadcasted_iota(jnp.int32, one.shape, 0) < 3
    out = []
    row = row_place()
    above = (jnp.where(even, two, one), row > 0)
    below = (jnp.where(even, one, two), row < rows - 1)
    for got, there in (above, below):
        keep = near & there
        out.append((jnp.where(keep, got, 0.0), jnp.where(keep, pltpu.roll(got, 4, 0), 0.0)))
    return out


def edges(rows, low_in, high_in, even_rows, odd_rows, totals, even_cols, odd_cols, low, high):
    low[...] = low_in[...]
    high[...] = high_in[...]
    for level in range(1, LEVELS + 1):
        tile, turn = HIGH[level], TURN[level]
        for at, (num, den) in zip((0, N[level]), from_rows(rows, even_rows, odd_rows, level)):
            for which, row, size, slot, place in PIECES:
                if which == level and row <= at < row + size:
                    to = slice(place + at - row, place + at - row + 8)
                    low[to, :] += three(num[:, 0:128], den[:, 0:128], slot)
                    num, den = (roll(x[:, tile : tile + 128], turn, 1) for x in (num, den))
                    high[to, :] += three(num, den, slot)
    even = lax.axis_index(COLS) % 2 == 0
    one, two = low[...], high[...]
    even_cols[0:SLOT, :] = jnp.where(even, two, one)
    odd_cols[0:SLOT, :] = jnp.where(even, one, two)
    even_cols[SLOT:, :] = totals[...]


def collapse(rows, cols, gains, l1, l2, l3, l4, l5, l6, even_rows, odd_rows, even_cols, odd_cols, wider, last, shifted, out, tall, wide, full):
    levels = (l1, l2, l3, l4, l5, l6)
    first_of_pair = lax.axis_index(COLS) % 2 == 0
    gain = [gains[k : k + 1, 0:1] for k in range(LEVELS)]

    def ratio(level):
        size, n, high = R[level], N[level], HIGH[level] // 128
        ref = levels[level - 1]
        strips = from_rows(rows, even_rows, odd_rows, level)
        for arr in range(2):
            store(full, arr, slice(0, size), load(ref, arr, slice(8, 8 + size)))
            for first, pair in zip((0, n), strips):
                for tile in range(W[level] // 128):
                    full[arr, tile, first : first + 8, :] += pair[arr][:, 128 * tile : 128 * tile + 128]
        for which, row, count, slot, place in PIECES:
            if which != level:
                continue
            one, two = even_cols[place : place + count, :], odd_cols[place : place + count, :]
            below = jnp.where(first_of_pair, two, one)
            above = jnp.where(first_of_pair, one, two)
            lane = lax.broadcasted_iota(jnp.int32, one.shape, 1)
            for arr in range(2):
                at = 8 * slot + 64 * arr
                low = jnp.where(lane < 3, roll(below, -at, 1), 0.0)
                up = n % 128
                up = jnp.where((lane >= up) & (lane < up + 3), roll(above, n - at, 1), 0.0)
                full[arr, 0, row : row + count, :] += low
                full[arr, high, row : row + count, :] += up
        mask = in_grid((size, W[level]), n, rows, cols)
        num, den = (load(full, arr, slice(0, size))[:, : W[level]] for arr in range(2))
        return mask, jnp.where(mask, num / jnp.where(mask, den, 1.0), 0.0)

    mask, value = ratio(LEVELS)
    piece = jnp.where(mask, -gain[LEVELS - 1] * value, 0.0)
    for level in range(LEVELS - 1, 0, -1):
        size, half = R[level], R[level] // 2
        tall[0 : R[level + 1], 0 : W[level]] = times(piece, wider[: W[level + 1], : W[level]])
        a, b, c = (tall[k : k + half, 0 : W[level]] for k in range(3))
        mask, value = ratio(level)
        even, odd = 0.5 * (a + b), 0.125 * (a + c) + 0.75 * b
        for tile in range(W[level] // 128):
            lanes = slice(128 * tile, 128 * tile + 128)
            wide[tile, pl.ds(0, half, stride=2), :] = even[:, lanes]
            wide[tile, pl.ds(1, half, stride=2), :] = odd[:, lanes]
        grown = jnp.concatenate([wide[tile, 0:size, :] for tile in range(W[level] // 128)], axis=1)
        change = gain[level] - gain[level - 1]
        piece = jnp.where(mask, change * value + grown, 0.0)
    tall[:, 0:256] = times(piece[:, 0:256], last[0:256, 0:256])
    tall[:, 256:512] = times(piece[:, 128:384], last[128:384, 256:512])
    half = TILE // 2
    for tile in range(W[0] // 128):
        lanes = slice(128 * tile, 128 * tile + 128)
        a, b, c = (tall[k : k + half, lanes] for k in range(3))
        wide[tile, pl.ds(0, half, stride=2), :] = 0.125 * (a + c) + 0.75 * b
        wide[tile, pl.ds(1, half, stride=2), :] = 0.5 * (b + c)
        out[:, lanes] = gain[0] * shifted[:, lanes] + wide[tile, :, :]


def finish(rest, ups, downs, totals, out, done, sems):
    mean = totals[0:1, 0:1] / totals[0:1, 64:65]
    part = TILE // PARTS
    copies = []
    for k in range(PARTS):
        at = slice(k * part, k * part + part)
        up = mean * ups[at, :]
        for tile in range(W[0] // 128):
            lanes = slice(128 * tile, 128 * tile + 128)
            done[at, lanes] = rest[at, lanes] + up * downs[0:1, lanes]
        copies.append(pltpu.make_async_copy(done.at[at], out.at[at], sems.at[k]))
        copies[-1].start()
    for copy in copies:
        copy.wait()


def swaps(count, first):
    return [p for i in range(first, count - 1, 2) for p in ((i, i + 1), (i + 1, i))]


def solution(mesh):
    rows, cols = mesh.shape["gy"] * mesh.shape["gz"], mesh.shape["gx"]
    wider = expand_matrix(W[2], W[1], 0)
    last = expand_matrix(W[1], W[0], 1)
    f32 = jnp.float32
    anyw, vmem = pl.BlockSpec(memory_space=pltpu.HBM), pl.BlockSpec(memory_space=pltpu.VMEM)
    params = pltpu.CompilerParams(vmem_limit_bytes=VMEM)
    stored = [jax.ShapeDtypeStruct((2, W[level] // 128, A[level], 128), f32) for level in range(1, LEVELS + 1)]
    block = jax.ShapeDtypeStruct((SLOT, 128), f32)
    strip = jax.ShapeDtypeStruct((8, STRIPS), f32)
    small = jax.ShapeDtypeStruct((8, 128), f32)
    tile = jax.ShapeDtypeStruct((TILE, TILE), f32)

    def ring(axis, size, unit=1):
        def at(i, j):
            return [(i * unit + u, j * unit + u) for u in range(unit)]

        def both(pairs):
            return [p for i, j in pairs for p in at(i, j) + at(j, i)]

        rounds = []
        if size > 1:
            rounds.append(both([(i, i + 1) for i in range(0, size, 2)]))
        if size == 4:
            rounds.append(both([(0, 3), (1, 2)]))
        if size == 8:
            rounds.append(both([(0, 2), (1, 3), (4, 6), (5, 7)]))
            rounds.append(both([(i, 7 - i) for i in range(4)]))
        return [(axis, r) for r in rounds]

    def add(totals, rounds):
        for axis, pairs in rounds:
            totals = totals + lax.ppermute(totals, axis, pairs)
        return totals

    gy, gz, gx = ring("gy", mesh.shape["gy"]), ring("gz", mesh.shape["gz"]), ring(COLS, cols // 2, 2)

    def local(heights, ids, offset, weight, gain):
        tables = jnp.concatenate([offset, weight, gain])
        *base, shifted, totals, gains, ups, downs = pl.pallas_call(
            lambda *refs: scenes(rows, cols, *refs),
            out_shape=[jax.ShapeDtypeStruct((A[0], 128), f32)] * 8
            + [tile, small, small, jax.ShapeDtypeStruct((TILE, 128), f32), jax.ShapeDtypeStruct((8, TILE), f32)],
            in_specs=[anyw] * 3,
            out_specs=[vmem] * 13,
            scratch_shapes=[
                pltpu.VMEM((TILE, TILE), f32),
                pltpu.VMEM((TILE, TILE), jnp.int32),
                pltpu.VMEM((R[1], 128), f32),
                pltpu.VMEM((TILE, 128), f32),
                pltpu.SMEM((2 * SCENES + LEVELS,), f32),
                pltpu.SemaphoreType.DMA((1 + 2 * PARTS,)),
            ],
            compiler_params=pltpu.CompilerParams(vmem_limit_bytes=FIRST_VMEM),
            name="scenes",
        )(heights, ids, tables)
        totals = add(totals, gz[1:])
        *levels, even_rows, odd_rows = pl.pallas_call(
            lambda *refs: pyramid(rows, cols, *refs),
            out_shape=[*stored, strip, strip],
            in_specs=[vmem] * 8,
            out_specs=[vmem] * (LEVELS + 2),
            scratch_shapes=[
                pltpu.VMEM((W[0], W[1]), jnp.bfloat16),
                pltpu.VMEM((W[1], W[2]), jnp.bfloat16),
            ],
            compiler_params=params,
            name="pyramid",
        )(*base)
        low, high = pl.pallas_call(
            pack,
            out_shape=[block, block],
            in_specs=[vmem] * LEVELS,
            out_specs=[vmem] * 2,
            compiler_params=params,
            name="pack",
        )(*levels)
        even_rows = jnp.concatenate([even_rows, totals], axis=1)
        even_rows = lax.ppermute(even_rows, ROWS, swaps(rows, 0))
        odd_rows = lax.ppermute(odd_rows, ROWS, swaps(rows, 1))
        totals = add(totals + even_rows[:, STRIPS:], gy[:1])
        even_cols, odd_cols = pl.pallas_call(
            lambda *refs: edges(rows, *refs),
            out_shape=[jax.ShapeDtypeStruct((SLOT + 8, 128), f32), block],
            in_specs=[vmem] * 5,
            out_specs=[vmem] * 2,
            scratch_shapes=[pltpu.VMEM((SLOT, 128), f32)] * 2,
            compiler_params=params,
            name="edges",
        )(low, high, even_rows, odd_rows, totals)
        even_cols = lax.ppermute(even_cols, COLS, swaps(cols, 0))
        totals, odd_cols = lax.optimization_barrier((totals + even_cols[SLOT:], odd_cols))
        for axis, pairs in gx[:1]:
            totals = totals + lax.ppermute(jnp.tile(totals, (BIG, 1)), axis, pairs)[0:8]
        totals = add(totals, gx[1:2] + gy[1:])
        odd_cols = lax.ppermute(odd_cols, COLS, swaps(cols, 1))
        rest = pl.pallas_call(
            lambda *refs: collapse(rows, cols, *refs),
            out_shape=tile,
            in_specs=[vmem] * 14,
            out_specs=vmem,
            scratch_shapes=[pltpu.VMEM((R[1], TILE), f32), pltpu.VMEM((W[0] // 128, TILE, 128), f32)]
            + [pltpu.VMEM((2, W[1] // 128, R[1], 128), f32)],
            compiler_params=params,
            name="collapse",
        )(gains, *levels, even_rows, odd_rows, even_cols, odd_cols, wider, last, shifted)
        totals, rest = lax.optimization_barrier((totals, rest))
        totals = add(totals, gx[2:])
        return pl.pallas_call(
            finish,
            out_shape=tile,
            in_specs=[vmem] * 4,
            out_specs=pl.BlockSpec(memory_space=pl.ANY),
            scratch_shapes=[pltpu.VMEM((TILE, TILE), f32), pltpu.SemaphoreType.DMA((PARTS,))],
            compiler_params=params,
            name="finish",
        )(rest, ups, downs, totals)

    spec = P(ROWS, COLS)
    return jax.shard_map(
        local, mesh=mesh, in_specs=(spec, spec, P(), P(), P()), out_specs=spec, check_vma=False
    )
```

```python
import jax
import jax.numpy as jnp
import numpy as np
from jax import lax
from jax.experimental import pallas as pl
from jax.experimental.pallas import tpu as pltpu
from jax.sharding import PartitionSpec as P

SCENES = 16
LEVELS = 6
TILE = 512
KERN = (0.0625, 0.25, 0.375, 0.25, 0.0625)
ROWS = ("gy", "gz")
COLS = "gx"

N = [TILE >> level for level in range(LEVELS + 1)]
R = [0, 272, 144, 80, 48, 32, 32]
A = [560, 304, 176, 112, 80, 80, 40]
W = [512, 384, 256, 128, 128, 128, 128]
STRIP = [0, 0, 384, 640, 768, 896, 1024]
STRIPS = 1152
SLOT = 80
PIECES = [
    (1, 0, 80, 0, 0),
    (1, 80, 80, 1, 0),
    (1, 160, 80, 2, 0),
    (1, 240, 32, 3, 0),
    (6, 0, 32, 3, 32),
    (2, 0, 80, 4, 0),
    (2, 80, 64, 5, 0),
    (3, 0, 80, 6, 0),
    (4, 0, 48, 7, 0),
    (5, 0, 32, 7, 48),
]
HIGH = [0, 256, 128, 0, 0, 0, 0]
TURN = [0, 0, 0, 64, 96, 112, 120]
PARTS = 4
BIG = 11
VMEM = 40 * 1024 * 1024
FIRST_VMEM = 50 * 1024 * 1024


def reduce_matrix(rows, cols, shift):
    t = lax.broadcasted_iota(jnp.int32, (rows, cols), 0)
    s = lax.broadcasted_iota(jnp.int32, (rows, cols), 1)
    d = jnp.abs(t - 2 * s + shift)
    out = jnp.where(d == 2, KERN[0], 0.0)
    return jnp.where(d == 1, KERN[1], jnp.where(d == 0, KERN[2], out)).astype(jnp.bfloat16)


def expand_matrix(rows, cols, shift):
    out = np.zeros((rows, cols), np.float32)
    for c in range(cols):
        s = c + shift
        j = s // 2
        taps = ((j, 0.5), (j + 1, 0.5)) if s % 2 == 0 else ((j, 0.125), (j + 1, 0.75), (j + 2, 0.125))
        for t, value in taps:
            if 0 <= t < rows:
                out[t, c] = value
    return out.astype(jnp.bfloat16)


def times(x, matrix):
    hi = x.astype(jnp.bfloat16)
    rest = x - hi.astype(jnp.float32)
    mid = rest.astype(jnp.bfloat16)
    lo = (rest - mid.astype(jnp.float32)).astype(jnp.bfloat16)
    out = jnp.dot(hi, matrix, preferred_element_type=jnp.float32)
    out = out + jnp.dot(mid, matrix, preferred_element_type=jnp.float32)
    return out + jnp.dot(lo, matrix, preferred_element_type=jnp.float32)


def load(ref, arr, at):
    return jnp.concatenate([ref[arr, tile, at, :] for tile in range(ref.shape[1])], axis=1)


def store(ref, arr, at, value):
    for tile in range(value.shape[1] // 128):
        ref[arr, tile, at, :] = value[:, 128 * tile : 128 * tile + 128]


def row_place():
    return lax.axis_index("gy") * lax.axis_size("gz") + lax.axis_index("gz")


def in_grid(shape, n, rows, cols):
    def side(dim, place, count):
        s = lax.broadcasted_iota(jnp.int32, shape, dim)
        low = jnp.where(place == 0, 1, 0)
        high = jnp.where(place == count - 1, n, n + 2)
        return (s >= low) & (s <= high)

    return side(0, row_place(), rows) & side(1, lax.axis_index(COLS), cols)


def roll(x, shift, axis):
    return pltpu.roll(x, shift % x.shape[axis], axis) if shift % x.shape[axis] else x


def three(num, den, low_slot):
    lane = lax.broadcasted_iota(jnp.int32, num.shape, 1)
    at = 8 * low_slot
    num = jnp.where((lane >= at) & (lane < at + 3), roll(num, at, 1), 0.0)
    return jnp.where((lane >= at + 64) & (lane < at + 67), roll(den, at + 64, 1), num)


def ones_expanded(place, count, tall, wide):
    for level in range(LEVELS, 0, -1):
        s = lax.broadcasted_iota(jnp.int32, (R[level], 128), 0)
        inside = (s >= jnp.where(place == 0, 1, 0)) & (s <= jnp.where(place == count - 1, N[level], N[level] + 2))
        x = 1.0 if level == LEVELS else wide[0 : R[level], :]
        tall[0 : R[level], :] = jnp.where(inside, x, 0.0)
        half = R[level - 1] // 2 if level > 1 else TILE // 2
        a, b, c = (tall[k : k + half, :] for k in range(3))
        even, odd = 0.5 * (a + b), 0.125 * (a + c) + 0.75 * b
        if level == 1:
            even, odd = odd, 0.5 * (b + c)
        wide[pl.ds(0, half, stride=2), :] = even
        wide[pl.ds(1, half, stride=2), :] = odd


def scenes(rows, cols, heights_in, ids_in, tables, *refs):
    base, (shifted, totals, gains, ups, downs, heights, ids, tall, wide, table, sems) = refs[:8], refs[8:]
    step, part = 64, TILE // PARTS
    pairs = [(tables, table)]
    for k in range(PARTS):
        at = slice(k * part, k * part + part)
        pairs.append((heights_in.at[at], heights.at[at]))
        pairs.append((ids_in.at[at], ids.at[at]))
    copies = [pltpu.make_async_copy(a, b, sems.at[k]) for k, (a, b) in enumerate(pairs)]
    for copy in copies:
        copy.start()
    for ref in base:
        ref[0:8, :] = jnp.zeros((8, 128), jnp.float32)
        ref[8 + TILE :, :] = jnp.zeros((A[0] - 8 - TILE, 128), jnp.float32)
    ones_expanded(lax.axis_index(COLS), cols, tall, wide)
    for tile in range(4):
        downs[:, 128 * tile : 128 * tile + 128] = wide[128 * tile : 128 * tile + 128, :].T[0:8, :]
    ones_expanded(row_place(), rows, tall, wide)
    ups[...] = wide[...]

    def cells(i, sums):
        at = pl.ds(pl.multiple_of(i * step, step), step)
        to = pl.ds(pl.multiple_of(i * step + 8, 8), step)
        which = ids[at, :]
        bits = [(which & (1 << b)) != 0 for b in range(4)]

        def lookup(first):
            values = [table[first + s] for s in range(SCENES)]
            for b in range(4):
                values = [
                    jnp.where(bits[b], values[2 * k + 1], values[2 * k]) for k in range(len(values) // 2)
                ]
            return values[0]

        tiles = [which[:, 128 * t : 128 * t + 128] for t in range(W[0] // 128)]
        tiles = [jnp.take_along_axis(weights, t, axis=1, mode="promise_in_bounds") for t in tiles]
        w = jnp.concatenate(tiles, axis=1)
        h = heights[at, :] + lookup(0)
        shifted[at, :] = h
        up = ups[at, :]
        up = jnp.concatenate([up] * (W[0] // 128), axis=1)
        out = []
        for arr, value in enumerate((w * h, w)):
            for tile in range(W[0] // 128):
                base[4 * arr + tile][to, :] = value[:, 128 * tile : 128 * tile + 128]
            value = value * up
            out.append(sums[arr] + sum(value[8 * k : 8 * k + 8] for k in range(step // 8)))
        return tuple(out)

    copies[0].wait()
    lane = lax.broadcasted_iota(jnp.int32, (step, 128), 1)
    weights = jnp.zeros((step, 128), jnp.float32)
    for s in range(SCENES):
        weights = jnp.where(lane == s, table[SCENES + s], weights)
    sums = (jnp.zeros((8, TILE), jnp.float32),) * 2
    for k in range(PARTS):
        copies[1 + 2 * k].wait()
        copies[2 + 2 * k].wait()
        sums = lax.fori_loop(k * part // step, (k + 1) * part // step, cells, sums)
    sums = [jnp.sum(x * downs[...]) for x in sums]
    lane = lax.broadcasted_iota(jnp.int32, (8, 128), 1)
    sub = lax.broadcasted_iota(jnp.int32, (8, 128), 0)
    totals[...] = jnp.where(lane < 64, sums[0], sums[1])
    gains[...] = sum(jnp.where(sub == k, table[2 * SCENES + k], 0.0) for k in range(LEVELS))


def pyramid(rows, cols, *refs):
    base, refs = refs[:8], refs[8:]
    levels, (even_rows, odd_rows, first, later) = refs[:LEVELS], refs[LEVELS:]
    first[...] = reduce_matrix(W[0], W[1], 2)
    later[...] = reduce_matrix(W[1], W[2], 1)
    for level in range(1, LEVELS + 1):
        target = levels[level - 1]
        start = 4 if level == 1 else 5
        size = R[level]
        matrix = first[...] if level == 1 else later[: W[level - 1], : W[level]]
        mask = in_grid((size, W[level]), N[level], rows, cols)
        for arr in range(2):
            places = [pl.ds(start + k, size, stride=2) for k in range(5)]
            if level == 1:
                taps = [jnp.concatenate([base[4 * arr + t][at, :] for t in range(4)], axis=1) for at in places]
            else:
                taps = [load(levels[level - 2], arr, at) for at in places]
            tall = KERN[0] * (taps[0] + taps[4]) + KERN[1] * (taps[1] + taps[3]) + KERN[2] * taps[2]
            if level == 1:
                part = [times(tall, matrix[:, 0:256]), times(tall[:, 384:512], matrix[384:512, 256:384])]
                part = jnp.concatenate(part, axis=1)
            else:
                part = times(tall, matrix)
            part = jnp.where(mask, part, 0.0)
            store(target, arr, slice(0, 8), jnp.zeros((8, W[level]), jnp.float32))
            store(target, arr, slice(8, 8 + size), part)
            if A[level] > 8 + size:
                rest = A[level] - 8 - size
                store(target, arr, slice(8 + size, A[level]), jnp.zeros((rest, W[level]), jnp.float32))

    even = row_place() % 2 == 0
    def strips(level, at):
        ref = levels[level - 1]
        num = load(ref, 0, slice(at, at + 8))
        den = pltpu.roll(load(ref, 1, slice(at, at + 8)), 4, 0)
        sub = lax.broadcasted_iota(jnp.int32, num.shape, 0)
        return jnp.where(sub < 3, num, jnp.where((sub > 3) & (sub < 7), den, 0.0))

    for level in range(1, LEVELS + 1):
        low, high = strips(level, 8), strips(level, 8 + N[level])
        to = slice(STRIP[level], STRIP[level] + W[level])
        even_rows[:, to] = jnp.where(even, high, low)
        odd_rows[:, to] = jnp.where(even, low, high)


def pack(*refs):
    levels, (low_cols, high_cols) = refs[:LEVELS], refs[LEVELS:]
    low_cols[...] = jnp.zeros(low_cols.shape, jnp.float32)
    high_cols[...] = jnp.zeros(high_cols.shape, jnp.float32)
    for level, row, size, slot, place in PIECES:
        tile, turn = HIGH[level] // 128, TURN[level]
        num, den = levels[level - 1].at[0], levels[level - 1].at[1]
        at, to = slice(8 + row, 8 + row + size), slice(place, place + size)
        low_cols[to, :] += three(num[0, at, :], den[0, at, :], slot)
        high_cols[to, :] += three(roll(num[tile, at, :], turn, 1), roll(den[tile, at, :], turn, 1), slot)


def from_rows(rows, even_rows, odd_rows, level):
    even = row_place() % 2 == 0
    to = slice(STRIP[level], STRIP[level] + W[level])
    one, two = even_rows[:, to], odd_rows[:, to]
    near = lax.broadcasted_iota(jnp.int32, one.shape, 0) < 3
    out = []
    row = row_place()
    above = (jnp.where(even, two, one), row > 0)
    below = (jnp.where(even, one, two), row < rows - 1)
    for got, there in (above, below):
        keep = near & there
        out.append((jnp.where(keep, got, 0.0), jnp.where(keep, pltpu.roll(got, 4, 0), 0.0)))
    return out


def edges(rows, low_in, high_in, even_rows, odd_rows, totals, even_cols, odd_cols, low, high):
    low[...] = low_in[...]
    high[...] = high_in[...]
    for level in range(1, LEVELS + 1):
        tile, turn = HIGH[level], TURN[level]
        for at, (num, den) in zip((0, N[level]), from_rows(rows, even_rows, odd_rows, level)):
            for which, row, size, slot, place in PIECES:
                if which == level and row <= at < row + size:
                    to = slice(place + at - row, place + at - row + 8)
                    low[to, :] += three(num[:, 0:128], den[:, 0:128], slot)
                    num, den = (roll(x[:, tile : tile + 128], turn, 1) for x in (num, den))
                    high[to, :] += three(num, den, slot)
    even = lax.axis_index(COLS) % 2 == 0
    one, two = low[...], high[...]
    even_cols[0:SLOT, :] = jnp.where(even, two, one)
    odd_cols[0:SLOT, :] = jnp.where(even, one, two)
    even_cols[SLOT:, :] = totals[...]


def collapse(rows, cols, gains, l1, l2, l3, l4, l5, l6, even_rows, odd_rows, even_cols, odd_cols, wider, last, shifted, out, tall, wide, full):
    levels = (l1, l2, l3, l4, l5, l6)
    first_of_pair = lax.axis_index(COLS) % 2 == 0
    gain = [gains[k : k + 1, 0:1] for k in range(LEVELS)]

    def ratio(level):
        size, n, high = R[level], N[level], HIGH[level] // 128
        ref = levels[level - 1]
        strips = from_rows(rows, even_rows, odd_rows, level)
        for arr in range(2):
            store(full, arr, slice(0, size), load(ref, arr, slice(8, 8 + size)))
            for first, pair in zip((0, n), strips):
                for tile in range(W[level] // 128):
                    full[arr, tile, first : first + 8, :] += pair[arr][:, 128 * tile : 128 * tile + 128]
        for which, row, count, slot, place in PIECES:
            if which != level:
                continue
            one, two = even_cols[place : place + count, :], odd_cols[place : place + count, :]
            below = jnp.where(first_of_pair, two, one)
            above = jnp.where(first_of_pair, one, two)
            lane = lax.broadcasted_iota(jnp.int32, one.shape, 1)
            for arr in range(2):
                at = 8 * slot + 64 * arr
                low = jnp.where(lane < 3, roll(below, -at, 1), 0.0)
                up = n % 128
                up = jnp.where((lane >= up) & (lane < up + 3), roll(above, n - at, 1), 0.0)
                full[arr, 0, row : row + count, :] += low
                full[arr, high, row : row + count, :] += up
        mask = in_grid((size, W[level]), n, rows, cols)
        num, den = (load(full, arr, slice(0, size))[:, : W[level]] for arr in range(2))
        return mask, jnp.where(mask, num / jnp.where(mask, den, 1.0), 0.0)

    mask, value = ratio(LEVELS)
    piece = jnp.where(mask, -gain[LEVELS - 1] * value, 0.0)
    for level in range(LEVELS - 1, 0, -1):
        size, half = R[level], R[level] // 2
        tall[0 : R[level + 1], 0 : W[level]] = times(piece, wider[: W[level + 1], : W[level]])
        a, b, c = (tall[k : k + half, 0 : W[level]] for k in range(3))
        mask, value = ratio(level)
        even, odd = 0.5 * (a + b), 0.125 * (a + c) + 0.75 * b
        for tile in range(W[level] // 128):
            lanes = slice(128 * tile, 128 * tile + 128)
            wide[tile, pl.ds(0, half, stride=2), :] = even[:, lanes]
            wide[tile, pl.ds(1, half, stride=2), :] = odd[:, lanes]
        grown = jnp.concatenate([wide[tile, 0:size, :] for tile in range(W[level] // 128)], axis=1)
        change = gain[level] - gain[level - 1]
        piece = jnp.where(mask, change * value + grown, 0.0)
    tall[:, 0:256] = times(piece[:, 0:256], last[0:256, 0:256])
    tall[:, 256:512] = times(piece[:, 128:384], last[128:384, 256:512])
    half = TILE // 2
    for tile in range(W[0] // 128):
        lanes = slice(128 * tile, 128 * tile + 128)
        a, b, c = (tall[k : k + half, lanes] for k in range(3))
        wide[tile, pl.ds(0, half, stride=2), :] = 0.125 * (a + c) + 0.75 * b
        wide[tile, pl.ds(1, half, stride=2), :] = 0.5 * (b + c)
        out[:, lanes] = gain[0] * shifted[:, lanes] + wide[tile, :, :]


def finish(rest, ups, downs, totals, out, done, sems):
    mean = totals[0:1, 0:1] / totals[0:1, 64:65]
    part = TILE // PARTS
    copies = []
    for k in range(PARTS):
        at = slice(k * part, k * part + part)
        up = mean * ups[at, :]
        for tile in range(W[0] // 128):
            lanes = slice(128 * tile, 128 * tile + 128)
            done[at, lanes] = rest[at, lanes] + up * downs[0:1, lanes]
        copies.append(pltpu.make_async_copy(done.at[at], out.at[at], sems.at[k]))
        copies[-1].start()
    for copy in copies:
        copy.wait()


def swaps(count, first):
    return [p for i in range(first, count - 1, 2) for p in ((i, i + 1), (i + 1, i))]


def solution(mesh):
    rows, cols = mesh.shape["gy"] * mesh.shape["gz"], mesh.shape["gx"]
    wider = expand_matrix(W[2], W[1], 0)
    last = expand_matrix(W[1], W[0], 1)
    f32 = jnp.float32
    anyw, vmem = pl.BlockSpec(memory_space=pltpu.HBM), pl.BlockSpec(memory_space=pltpu.VMEM)
    params = pltpu.CompilerParams(vmem_limit_bytes=VMEM)
    stored = [jax.ShapeDtypeStruct((2, W[level] // 128, A[level], 128), f32) for level in range(1, LEVELS + 1)]
    block = jax.ShapeDtypeStruct((SLOT, 128), f32)
    strip = jax.ShapeDtypeStruct((8, STRIPS), f32)
    small = jax.ShapeDtypeStruct((8, 128), f32)
    tile = jax.ShapeDtypeStruct((TILE, TILE), f32)

    def ring(axis, size, unit=1):
        def at(i, j):
            return [(i * unit + u, j * unit + u) for u in range(unit)]

        def both(pairs):
            return [p for i, j in pairs for p in at(i, j) + at(j, i)]

        rounds = []
        if size > 1:
            rounds.append(both([(i, i + 1) for i in range(0, size, 2)]))
        if size == 4:
            rounds.append(both([(0, 3), (1, 2)]))
        if size == 8:
            rounds.append(both([(0, 2), (1, 3), (4, 6), (5, 7)]))
            rounds.append(both([(i, 7 - i) for i in range(4)]))
        return [(axis, r) for r in rounds]

    def add(totals, rounds):
        for axis, pairs in rounds:
            totals = totals + lax.ppermute(totals, axis, pairs)
        return totals

    gy, gz, gx = ring("gy", mesh.shape["gy"]), ring("gz", mesh.shape["gz"]), ring(COLS, cols // 2, 2)

    def local(heights, ids, offset, weight, gain):
        tables = jnp.concatenate([offset, weight, gain])
        *base, shifted, totals, gains, ups, downs = pl.pallas_call(
            lambda *refs: scenes(rows, cols, *refs),
            out_shape=[jax.ShapeDtypeStruct((A[0], 128), f32)] * 8
            + [tile, small, small, jax.ShapeDtypeStruct((TILE, 128), f32), jax.ShapeDtypeStruct((8, TILE), f32)],
            in_specs=[anyw] * 3,
            out_specs=[vmem] * 13,
            scratch_shapes=[
                pltpu.VMEM((TILE, TILE), f32),
                pltpu.VMEM((TILE, TILE), jnp.int32),
                pltpu.VMEM((R[1], 128), f32),
                pltpu.VMEM((TILE, 128), f32),
                pltpu.SMEM((2 * SCENES + LEVELS,), f32),
                pltpu.SemaphoreType.DMA((1 + 2 * PARTS,)),
            ],
            compiler_params=pltpu.CompilerParams(vmem_limit_bytes=FIRST_VMEM),
            name="scenes",
        )(heights, ids, tables)
        totals = add(totals, gz[1:])
        *levels, even_rows, odd_rows = pl.pallas_call(
            lambda *refs: pyramid(rows, cols, *refs),
            out_shape=[*stored, strip, strip],
            in_specs=[vmem] * 8,
            out_specs=[vmem] * (LEVELS + 2),
            scratch_shapes=[
                pltpu.VMEM((W[0], W[1]), jnp.bfloat16),
                pltpu.VMEM((W[1], W[2]), jnp.bfloat16),
            ],
            compiler_params=params,
            name="pyramid",
        )(*base)
        low, high = pl.pallas_call(
            pack,
            out_shape=[block, block],
            in_specs=[vmem] * LEVELS,
            out_specs=[vmem] * 2,
            compiler_params=params,
            name="pack",
        )(*levels)
        even_rows = jnp.concatenate([even_rows, totals], axis=1)
        even_rows = lax.ppermute(even_rows, ROWS, swaps(rows, 0))
        odd_rows = lax.ppermute(odd_rows, ROWS, swaps(rows, 1))
        totals = add(totals + even_rows[:, STRIPS:], gy[:1])
        even_cols, odd_cols = pl.pallas_call(
            lambda *refs: edges(rows, *refs),
            out_shape=[jax.ShapeDtypeStruct((SLOT + 8, 128), f32), block],
            in_specs=[vmem] * 5,
            out_specs=[vmem] * 2,
            scratch_shapes=[pltpu.VMEM((SLOT, 128), f32)] * 2,
            compiler_params=params,
            name="edges",
        )(low, high, even_rows, odd_rows, totals)
        even_cols = lax.ppermute(even_cols, COLS, swaps(cols, 0))
        totals, odd_cols = lax.optimization_barrier((totals + even_cols[SLOT:], odd_cols))
        for axis, pairs in gx[:1]:
            totals = totals + lax.ppermute(jnp.tile(totals, (BIG, 1)), axis, pairs)[0:8]
        totals = add(totals, gy[1:] + gx[1:2])
        odd_cols = lax.ppermute(odd_cols, COLS, swaps(cols, 1))
        rest = pl.pallas_call(
            lambda *refs: collapse(rows, cols, *refs),
            out_shape=tile,
            in_specs=[vmem] * 14,
            out_specs=vmem,
            scratch_shapes=[pltpu.VMEM((R[1], TILE), f32), pltpu.VMEM((W[0] // 128, TILE, 128), f32)]
            + [pltpu.VMEM((2, W[1] // 128, R[1], 128), f32)],
            compiler_params=params,
            name="collapse",
        )(gains, *levels, even_rows, odd_rows, even_cols, odd_cols, wider, last, shifted)
        totals, rest = lax.optimization_barrier((totals, rest))
        totals = add(totals, gx[2:])
        return pl.pallas_call(
            finish,
            out_shape=tile,
            in_specs=[vmem] * 4,
            out_specs=pl.BlockSpec(memory_space=pl.ANY),
            scratch_shapes=[pltpu.VMEM((TILE, TILE), f32), pltpu.SemaphoreType.DMA((PARTS,))],
            compiler_params=params,
            name="finish",
        )(rest, ups, downs, totals)

    spec = P(ROWS, COLS)
    return jax.shard_map(
        local, mesh=mesh, in_specs=(spec, spec, P(), P(), P()), out_specs=spec, check_vma=False
    )
```

```python
import jax
import jax.numpy as jnp
import numpy as np
from jax import lax
from jax.experimental import pallas as pl
from jax.experimental.pallas import tpu as pltpu
from jax.sharding import PartitionSpec as P

SCENES = 16
LEVELS = 6
TILE = 512
KERN = (0.0625, 0.25, 0.375, 0.25, 0.0625)
ROWS = ("gy", "gz")
COLS = "gx"

N = [TILE >> level for level in range(LEVELS + 1)]
R = [0, 272, 144, 80, 48, 32, 32]
A = [560, 304, 176, 112, 80, 80, 40]
W = [512, 384, 256, 128, 128, 128, 128]
STRIP = [0, 0, 384, 640, 768, 896, 1024]
STRIPS = 1152
SLOT = 80
PIECES = [
    (1, 0, 80, 0, 0),
    (1, 80, 80, 1, 0),
    (1, 160, 80, 2, 0),
    (1, 240, 32, 3, 0),
    (6, 0, 32, 3, 32),
    (2, 0, 80, 4, 0),
    (2, 80, 64, 5, 0),
    (3, 0, 80, 6, 0),
    (4, 0, 48, 7, 0),
    (5, 0, 32, 7, 48),
]
HIGH = [0, 256, 128, 0, 0, 0, 0]
TURN = [0, 0, 0, 64, 96, 112, 120]
PARTS = 4
BIG = 11
VMEM = 40 * 1024 * 1024
FIRST_VMEM = 50 * 1024 * 1024


def reduce_matrix(rows, cols, shift):
    t = lax.broadcasted_iota(jnp.int32, (rows, cols), 0)
    s = lax.broadcasted_iota(jnp.int32, (rows, cols), 1)
    d = jnp.abs(t - 2 * s + shift)
    out = jnp.where(d == 2, KERN[0], 0.0)
    return jnp.where(d == 1, KERN[1], jnp.where(d == 0, KERN[2], out)).astype(jnp.bfloat16)


def expand_matrix(rows, cols, shift):
    out = np.zeros((rows, cols), np.float32)
    for c in range(cols):
        s = c + shift
        j = s // 2
        taps = ((j, 0.5), (j + 1, 0.5)) if s % 2 == 0 else ((j, 0.125), (j + 1, 0.75), (j + 2, 0.125))
        for t, value in taps:
            if 0 <= t < rows:
                out[t, c] = value
    return out.astype(jnp.bfloat16)


def times(x, matrix):
    hi = x.astype(jnp.bfloat16)
    rest = x - hi.astype(jnp.float32)
    mid = rest.astype(jnp.bfloat16)
    lo = (rest - mid.astype(jnp.float32)).astype(jnp.bfloat16)
    out = jnp.dot(hi, matrix, preferred_element_type=jnp.float32)
    out = out + jnp.dot(mid, matrix, preferred_element_type=jnp.float32)
    return out + jnp.dot(lo, matrix, preferred_element_type=jnp.float32)


def load(ref, arr, at):
    return jnp.concatenate([ref[arr, tile, at, :] for tile in range(ref.shape[1])], axis=1)


def store(ref, arr, at, value):
    for tile in range(value.shape[1] // 128):
        ref[arr, tile, at, :] = value[:, 128 * tile : 128 * tile + 128]


def row_place():
    return lax.axis_index("gy") * lax.axis_size("gz") + lax.axis_index("gz")


def in_grid(shape, n, rows, cols):
    def side(dim, place, count):
        s = lax.broadcasted_iota(jnp.int32, shape, dim)
        low = jnp.where(place == 0, 1, 0)
        high = jnp.where(place == count - 1, n, n + 2)
        return (s >= low) & (s <= high)

    return side(0, row_place(), rows) & side(1, lax.axis_index(COLS), cols)


def roll(x, shift, axis):
    return pltpu.roll(x, shift % x.shape[axis], axis) if shift % x.shape[axis] else x


def three(num, den, low_slot):
    lane = lax.broadcasted_iota(jnp.int32, num.shape, 1)
    at = 8 * low_slot
    num = jnp.where((lane >= at) & (lane < at + 3), roll(num, at, 1), 0.0)
    return jnp.where((lane >= at + 64) & (lane < at + 67), roll(den, at + 64, 1), num)


def ones_expanded(place, count, tall, wide):
    for level in range(LEVELS, 0, -1):
        s = lax.broadcasted_iota(jnp.int32, (R[level], 128), 0)
        inside = (s >= jnp.where(place == 0, 1, 0)) & (s <= jnp.where(place == count - 1, N[level], N[level] + 2))
        x = 1.0 if level == LEVELS else wide[0 : R[level], :]
        tall[0 : R[level], :] = jnp.where(inside, x, 0.0)
        half = R[level - 1] // 2 if level > 1 else TILE // 2
        a, b, c = (tall[k : k + half, :] for k in range(3))
        even, odd = 0.5 * (a + b), 0.125 * (a + c) + 0.75 * b
        if level == 1:
            even, odd = odd, 0.5 * (b + c)
        wide[pl.ds(0, half, stride=2), :] = even
        wide[pl.ds(1, half, stride=2), :] = odd


def scenes(rows, cols, heights_in, ids_in, tables, *refs):
    base, (shifted, totals, gains, ups, downs, heights, ids, tall, wide, table, sems) = refs[:8], refs[8:]
    step, part = 128, TILE // PARTS
    pairs = [(tables, table)]
    for k in range(PARTS):
        at = slice(k * part, k * part + part)
        pairs.append((heights_in.at[at], heights.at[at]))
        pairs.append((ids_in.at[at], ids.at[at]))
    copies = [pltpu.make_async_copy(a, b, sems.at[k]) for k, (a, b) in enumerate(pairs)]
    for copy in copies:
        copy.start()
    for ref in base:
        ref[0:8, :] = jnp.zeros((8, 128), jnp.float32)
        ref[8 + TILE :, :] = jnp.zeros((A[0] - 8 - TILE, 128), jnp.float32)
    ones_expanded(lax.axis_index(COLS), cols, tall, wide)
    for tile in range(4):
        downs[:, 128 * tile : 128 * tile + 128] = wide[128 * tile : 128 * tile + 128, :].T[0:8, :]
    ones_expanded(row_place(), rows, tall, wide)
    ups[...] = wide[...]

    def cells(i, sums):
        at = pl.ds(pl.multiple_of(i * step, step), step)
        to = pl.ds(pl.multiple_of(i * step + 8, 8), step)
        which = ids[at, :]
        bits = [(which & (1 << b)) != 0 for b in range(4)]

        def lookup(first):
            values = [table[first + s] for s in range(SCENES)]
            for b in range(4):
                values = [
                    jnp.where(bits[b], values[2 * k + 1], values[2 * k]) for k in range(len(values) // 2)
                ]
            return values[0]

        tiles = [which[:, 128 * t : 128 * t + 128] for t in range(W[0] // 128)]
        tiles = [jnp.take_along_axis(weights, t, axis=1, mode="promise_in_bounds") for t in tiles]
        w = jnp.concatenate(tiles, axis=1)
        h = heights[at, :] + lookup(0)
        shifted[at, :] = h
        up = ups[at, :]
        up = jnp.concatenate([up] * (W[0] // 128), axis=1)
        out = []
        for arr, value in enumerate((w * h, w)):
            for tile in range(W[0] // 128):
                base[4 * arr + tile][to, :] = value[:, 128 * tile : 128 * tile + 128]
            value = value * up
            out.append(sums[arr] + sum(value[8 * k : 8 * k + 8] for k in range(step // 8)))
        return tuple(out)

    copies[0].wait()
    lane = lax.broadcasted_iota(jnp.int32, (step, 128), 1)
    weights = jnp.zeros((step, 128), jnp.float32)
    for s in range(SCENES):
        weights = jnp.where(lane == s, table[SCENES + s], weights)
    sums = (jnp.zeros((8, TILE), jnp.float32),) * 2
    for k in range(PARTS):
        copies[1 + 2 * k].wait()
        copies[2 + 2 * k].wait()
        sums = lax.fori_loop(k * part // step, (k + 1) * part // step, cells, sums)
    sums = [jnp.sum(x * downs[...]) for x in sums]
    lane = lax.broadcasted_iota(jnp.int32, (8, 128), 1)
    sub = lax.broadcasted_iota(jnp.int32, (8, 128), 0)
    totals[...] = jnp.where(lane < 64, sums[0], sums[1])
    gains[...] = sum(jnp.where(sub == k, table[2 * SCENES + k], 0.0) for k in range(LEVELS))


def pyramid(rows, cols, *refs):
    base, refs = refs[:8], refs[8:]
    levels, (even_rows, odd_rows, first, later) = refs[:LEVELS], refs[LEVELS:]
    first[...] = reduce_matrix(W[0], W[1], 2)
    later[...] = reduce_matrix(W[1], W[2], 1)
    for level in range(1, LEVELS + 1):
        target = levels[level - 1]
        start = 4 if level == 1 else 5
        size = R[level]
        matrix = first[...] if level == 1 else later[: W[level - 1], : W[level]]
        mask = in_grid((size, W[level]), N[level], rows, cols)
        for arr in range(2):
            places = [pl.ds(start + k, size, stride=2) for k in range(5)]
            if level == 1:
                taps = [jnp.concatenate([base[4 * arr + t][at, :] for t in range(4)], axis=1) for at in places]
            else:
                taps = [load(levels[level - 2], arr, at) for at in places]
            tall = KERN[0] * (taps[0] + taps[4]) + KERN[1] * (taps[1] + taps[3]) + KERN[2] * taps[2]
            if level == 1:
                part = [times(tall, matrix[:, 0:256]), times(tall[:, 384:512], matrix[384:512, 256:384])]
                part = jnp.concatenate(part, axis=1)
            else:
                part = times(tall, matrix)
            part = jnp.where(mask, part, 0.0)
            store(target, arr, slice(0, 8), jnp.zeros((8, W[level]), jnp.float32))
            store(target, arr, slice(8, 8 + size), part)
            if A[level] > 8 + size:
                rest = A[level] - 8 - size
                store(target, arr, slice(8 + size, A[level]), jnp.zeros((rest, W[level]), jnp.float32))

    even = row_place() % 2 == 0
    def strips(level, at):
        ref = levels[level - 1]
        num = load(ref, 0, slice(at, at + 8))
        den = pltpu.roll(load(ref, 1, slice(at, at + 8)), 4, 0)
        sub = lax.broadcasted_iota(jnp.int32, num.shape, 0)
        return jnp.where(sub < 3, num, jnp.where((sub > 3) & (sub < 7), den, 0.0))

    for level in range(1, LEVELS + 1):
        low, high = strips(level, 8), strips(level, 8 + N[level])
        to = slice(STRIP[level], STRIP[level] + W[level])
        even_rows[:, to] = jnp.where(even, high, low)
        odd_rows[:, to] = jnp.where(even, low, high)


def pack(*refs):
    levels, (low_cols, high_cols) = refs[:LEVELS], refs[LEVELS:]
    low_cols[...] = jnp.zeros(low_cols.shape, jnp.float32)
    high_cols[...] = jnp.zeros(high_cols.shape, jnp.float32)
    for level, row, size, slot, place in PIECES:
        tile, turn = HIGH[level] // 128, TURN[level]
        num, den = levels[level - 1].at[0], levels[level - 1].at[1]
        at, to = slice(8 + row, 8 + row + size), slice(place, place + size)
        low_cols[to, :] += three(num[0, at, :], den[0, at, :], slot)
        high_cols[to, :] += three(roll(num[tile, at, :], turn, 1), roll(den[tile, at, :], turn, 1), slot)


def from_rows(rows, even_rows, odd_rows, level):
    even = row_place() % 2 == 0
    to = slice(STRIP[level], STRIP[level] + W[level])
    one, two = even_rows[:, to], odd_rows[:, to]
    near = lax.broadcasted_iota(jnp.int32, one.shape, 0) < 3
    out = []
    row = row_place()
    above = (jnp.where(even, two, one), row > 0)
    below = (jnp.where(even, one, two), row < rows - 1)
    for got, there in (above, below):
        keep = near & there
        out.append((jnp.where(keep, got, 0.0), jnp.where(keep, pltpu.roll(got, 4, 0), 0.0)))
    return out


def edges(rows, low_in, high_in, even_rows, odd_rows, totals, even_cols, odd_cols, low, high):
    low[...] = low_in[...]
    high[...] = high_in[...]
    for level in range(1, LEVELS + 1):
        tile, turn = HIGH[level], TURN[level]
        for at, (num, den) in zip((0, N[level]), from_rows(rows, even_rows, odd_rows, level)):
            for which, row, size, slot, place in PIECES:
                if which == level and row <= at < row + size:
                    to = slice(place + at - row, place + at - row + 8)
                    low[to, :] += three(num[:, 0:128], den[:, 0:128], slot)
                    num, den = (roll(x[:, tile : tile + 128], turn, 1) for x in (num, den))
                    high[to, :] += three(num, den, slot)
    even = lax.axis_index(COLS) % 2 == 0
    one, two = low[...], high[...]
    even_cols[0:SLOT, :] = jnp.where(even, two, one)
    odd_cols[0:SLOT, :] = jnp.where(even, one, two)
    even_cols[SLOT:, :] = totals[...]


def collapse(rows, cols, gains, l1, l2, l3, l4, l5, l6, even_rows, odd_rows, even_cols, odd_cols, wider, last, shifted, out, tall, wide, full):
    levels = (l1, l2, l3, l4, l5, l6)
    first_of_pair = lax.axis_index(COLS) % 2 == 0
    gain = [gains[k : k + 1, 0:1] for k in range(LEVELS)]

    def ratio(level):
        size, n, high = R[level], N[level], HIGH[level] // 128
        ref = levels[level - 1]
        strips = from_rows(rows, even_rows, odd_rows, level)
        for arr in range(2):
            store(full, arr, slice(0, size), load(ref, arr, slice(8, 8 + size)))
            for first, pair in zip((0, n), strips):
                for tile in range(W[level] // 128):
                    full[arr, tile, first : first + 8, :] += pair[arr][:, 128 * tile : 128 * tile + 128]
        for which, row, count, slot, place in PIECES:
            if which != level:
                continue
            one, two = even_cols[place : place + count, :], odd_cols[place : place + count, :]
            below = jnp.where(first_of_pair, two, one)
            above = jnp.where(first_of_pair, one, two)
            lane = lax.broadcasted_iota(jnp.int32, one.shape, 1)
            for arr in range(2):
                at = 8 * slot + 64 * arr
                low = jnp.where(lane < 3, roll(below, -at, 1), 0.0)
                up = n % 128
                up = jnp.where((lane >= up) & (lane < up + 3), roll(above, n - at, 1), 0.0)
                full[arr, 0, row : row + count, :] += low
                full[arr, high, row : row + count, :] += up
        mask = in_grid((size, W[level]), n, rows, cols)
        num, den = (load(full, arr, slice(0, size))[:, : W[level]] for arr in range(2))
        return mask, jnp.where(mask, num / jnp.where(mask, den, 1.0), 0.0)

    mask, value = ratio(LEVELS)
    piece = jnp.where(mask, -gain[LEVELS - 1] * value, 0.0)
    for level in range(LEVELS - 1, 0, -1):
        size, half = R[level], R[level] // 2
        tall[0 : R[level + 1], 0 : W[level]] = times(piece, wider[: W[level + 1], : W[level]])
        a, b, c = (tall[k : k + half, 0 : W[level]] for k in range(3))
        mask, value = ratio(level)
        even, odd = 0.5 * (a + b), 0.125 * (a + c) + 0.75 * b
        for tile in range(W[level] // 128):
            lanes = slice(128 * tile, 128 * tile + 128)
            wide[tile, pl.ds(0, half, stride=2), :] = even[:, lanes]
            wide[tile, pl.ds(1, half, stride=2), :] = odd[:, lanes]
        grown = jnp.concatenate([wide[tile, 0:size, :] for tile in range(W[level] // 128)], axis=1)
        change = gain[level] - gain[level - 1]
        piece = jnp.where(mask, change * value + grown, 0.0)
    tall[:, 0:256] = times(piece[:, 0:256], last[0:256, 0:256])
    tall[:, 256:512] = times(piece[:, 128:384], last[128:384, 256:512])
    half = TILE // 2
    for tile in range(W[0] // 128):
        lanes = slice(128 * tile, 128 * tile + 128)
        a, b, c = (tall[k : k + half, lanes] for k in range(3))
        wide[tile, pl.ds(0, half, stride=2), :] = 0.125 * (a + c) + 0.75 * b
        wide[tile, pl.ds(1, half, stride=2), :] = 0.5 * (b + c)
        out[:, lanes] = gain[0] * shifted[:, lanes] + wide[tile, :, :]


def finish(rest, ups, downs, totals, out, done, sems):
    mean = totals[0:1, 0:1] / totals[0:1, 64:65]
    part = TILE // PARTS
    copies = []
    for k in range(PARTS):
        at = slice(k * part, k * part + part)
        up = mean * ups[at, :]
        for tile in range(W[0] // 128):
            lanes = slice(128 * tile, 128 * tile + 128)
            done[at, lanes] = rest[at, lanes] + up * downs[0:1, lanes]
        copies.append(pltpu.make_async_copy(done.at[at], out.at[at], sems.at[k]))
        copies[-1].start()
    for copy in copies:
        copy.wait()


def swaps(count, first):
    return [p for i in range(first, count - 1, 2) for p in ((i, i + 1), (i + 1, i))]


def solution(mesh):
    rows, cols = mesh.shape["gy"] * mesh.shape["gz"], mesh.shape["gx"]
    wider = expand_matrix(W[2], W[1], 0)
    last = expand_matrix(W[1], W[0], 1)
    f32 = jnp.float32
    anyw, vmem = pl.BlockSpec(memory_space=pltpu.HBM), pl.BlockSpec(memory_space=pltpu.VMEM)
    params = pltpu.CompilerParams(vmem_limit_bytes=VMEM)
    stored = [jax.ShapeDtypeStruct((2, W[level] // 128, A[level], 128), f32) for level in range(1, LEVELS + 1)]
    block = jax.ShapeDtypeStruct((SLOT, 128), f32)
    strip = jax.ShapeDtypeStruct((8, STRIPS), f32)
    small = jax.ShapeDtypeStruct((8, 128), f32)
    tile = jax.ShapeDtypeStruct((TILE, TILE), f32)

    def ring(axis, size, unit=1):
        def at(i, j):
            return [(i * unit + u, j * unit + u) for u in range(unit)]

        def both(pairs):
            return [p for i, j in pairs for p in at(i, j) + at(j, i)]

        rounds = []
        if size > 1:
            rounds.append(both([(i, i + 1) for i in range(0, size, 2)]))
        if size == 4:
            rounds.append(both([(0, 3), (1, 2)]))
        if size == 8:
            rounds.append(both([(0, 2), (1, 3), (4, 6), (5, 7)]))
            rounds.append(both([(i, 7 - i) for i in range(4)]))
        return [(axis, r) for r in rounds]

    def add(totals, rounds):
        for axis, pairs in rounds:
            totals = totals + lax.ppermute(totals, axis, pairs)
        return totals

    gy, gz, gx = ring("gy", mesh.shape["gy"]), ring("gz", mesh.shape["gz"]), ring(COLS, cols // 2, 2)

    def local(heights, ids, offset, weight, gain):
        tables = jnp.concatenate([offset, weight, gain])
        *base, shifted, totals, gains, ups, downs = pl.pallas_call(
            lambda *refs: scenes(rows, cols, *refs),
            out_shape=[jax.ShapeDtypeStruct((A[0], 128), f32)] * 8
            + [tile, small, small, jax.ShapeDtypeStruct((TILE, 128), f32), jax.ShapeDtypeStruct((8, TILE), f32)],
            in_specs=[anyw] * 3,
            out_specs=[vmem] * 13,
            scratch_shapes=[
                pltpu.VMEM((TILE, TILE), f32),
                pltpu.VMEM((TILE, TILE), jnp.int32),
                pltpu.VMEM((R[1], 128), f32),
                pltpu.VMEM((TILE, 128), f32),
                pltpu.SMEM((2 * SCENES + LEVELS,), f32),
                pltpu.SemaphoreType.DMA((1 + 2 * PARTS,)),
            ],
            compiler_params=pltpu.CompilerParams(vmem_limit_bytes=FIRST_VMEM),
            name="scenes",
        )(heights, ids, tables)
        totals = add(totals, gz[1:])
        *levels, even_rows, odd_rows = pl.pallas_call(
            lambda *refs: pyramid(rows, cols, *refs),
            out_shape=[*stored, strip, strip],
            in_specs=[vmem] * 8,
            out_specs=[vmem] * (LEVELS + 2),
            scratch_shapes=[
                pltpu.VMEM((W[0], W[1]), jnp.bfloat16),
                pltpu.VMEM((W[1], W[2]), jnp.bfloat16),
            ],
            compiler_params=params,
            name="pyramid",
        )(*base)
        low, high = pl.pallas_call(
            pack,
            out_shape=[block, block],
            in_specs=[vmem] * LEVELS,
            out_specs=[vmem] * 2,
            compiler_params=params,
            name="pack",
        )(*levels)
        even_rows = jnp.concatenate([even_rows, totals], axis=1)
        even_rows = lax.ppermute(even_rows, ROWS, swaps(rows, 0))
        odd_rows = lax.ppermute(odd_rows, ROWS, swaps(rows, 1))
        totals = add(totals + even_rows[:, STRIPS:], gy[:1])
        even_cols, odd_cols = pl.pallas_call(
            lambda *refs: edges(rows, *refs),
            out_shape=[jax.ShapeDtypeStruct((SLOT + 8, 128), f32), block],
            in_specs=[vmem] * 5,
            out_specs=[vmem] * 2,
            scratch_shapes=[pltpu.VMEM((SLOT, 128), f32)] * 2,
            compiler_params=params,
            name="edges",
        )(low, high, even_rows, odd_rows, totals)
        even_cols = lax.ppermute(even_cols, COLS, swaps(cols, 0))
        totals, odd_cols = lax.optimization_barrier((totals + even_cols[SLOT:], odd_cols))
        for axis, pairs in gx[:1]:
            totals = totals + lax.ppermute(jnp.tile(totals, (BIG, 1)), axis, pairs)[0:8]
        totals = add(totals, gy[1:] + gx[1:2])
        odd_cols = lax.ppermute(odd_cols, COLS, swaps(cols, 1))
        rest = pl.pallas_call(
            lambda *refs: collapse(rows, cols, *refs),
            out_shape=tile,
            in_specs=[vmem] * 14,
            out_specs=vmem,
            scratch_shapes=[pltpu.VMEM((R[1], TILE), f32), pltpu.VMEM((W[0] // 128, TILE, 128), f32)]
            + [pltpu.VMEM((2, W[1] // 128, R[1], 128), f32)],
            compiler_params=params,
            name="collapse",
        )(gains, *levels, even_rows, odd_rows, even_cols, odd_cols, wider, last, shifted)
        totals, rest = lax.optimization_barrier((totals, rest))
        totals = add(totals, gx[2:])
        return pl.pallas_call(
            finish,
            out_shape=tile,
            in_specs=[vmem] * 4,
            out_specs=pl.BlockSpec(memory_space=pl.ANY),
            scratch_shapes=[pltpu.VMEM((TILE, TILE), f32), pltpu.SemaphoreType.DMA((PARTS,))],
            compiler_params=params,
            name="finish",
        )(rest, ups, downs, totals)

    spec = P(ROWS, COLS)
    return jax.shard_map(
        local, mesh=mesh, in_specs=(spec, spec, P(), P(), P()), out_specs=spec, check_vma=False
    )
```
